256 devices in a mesh: aux: 64 (over z, y, x_lo), rows: 4 (over x_hi, core).
Axes of the slice: x: 4 (x_hi: 2, x_lo: 2; x = x_hi * 2 + x_lo), y: 4, z: 8, core: 2. Of those that a mesh axis runs over, the one named last changes fastest.
Arguments:
- half_ints: bfloat16 [192, 500, 4096], P('aux', None, 'rows'), may hold values from -0.109375 to 0.109375
Outputs:
- exchange_matrix: float32 [1024, 4, 4096], P('aux', None, 'rows')
The draws below stay inside these ranges and needn't reach their ends.
All inputs are finite; a program needn't handle non-finite values.
Results may differ from the reference program's by a relative error of at most 0.0023.
Values may be sent and summed in bfloat16 or wider, within the bound.
A program may use at most 192 MiB of HBM per device.

```python
import jax
import jax.numpy as jnp
from jax import lax

NBAS = 4096
OCC = 500
AUX = 192
N_ROWS = 4


def raised(result, own_key, source, target, parts, factor):
    def block_of(position):
        return (jnp.arange(result.shape[position]) // (result.shape[position] // parts)).reshape((-1,) + (1,) * (result.ndim - 1 - position))

    near = jax.random.permutation(own_key, parts)[block_of(target)]
    second = (block_of(target) + parts // 2) % parts
    return jnp.where((block_of(source) == near) | (block_of(source) == second), factor * result, result)


def shard_levels(key, shape, cuts, low, top_value):
    def one(axis_at, shards_of):
        heights = jax.random.uniform(jax.random.fold_in(jax.random.fold_in(key, 6), axis_at), (shards_of,), jnp.float32, low / len(cuts), top_value / len(cuts))
        return jnp.repeat(jnp.exp(heights), shape[axis_at] // shards_of).reshape((-1,) + (1,) * (len(shape) - axis_at - 1))

    level = one(*cuts[0])
    for cut in cuts[1:]:
        level = level * one(*cut)
    return level


def noise_with(stream_key, extent, deviation, reach, cuts, heavy, kind=jnp.bfloat16):
    values = deviation * jax.random.normal(stream_key, extent, jnp.float32)
    if cuts:
        values = values * shard_levels(stream_key, extent, cuts, -0.22, 0.18)
    return jnp.clip(raised(values, jax.random.fold_in(stream_key, 3), *heavy), -reach, reach).astype(kind)


def setup_inputs(seed: int = 0) -> dict:
    key_of = jax.random.split(jax.random.key(seed), 2)
    half_ints = noise_with(key_of[0], (AUX, OCC, NBAS), (AUX * OCC // 4) ** -0.5, 0.109375, ((0, 64), (2, 4)), (0, 2, 64, 4.0))
    return dict(half_ints=half_ints)


def reference(half_ints):
    def add_block(total, block):
        wide = block.astype(jnp.float32)
        product = jnp.dot(wide.T, wide, preferred_element_type=jnp.float32, precision=lax.Precision.HIGHEST)
        return total + product, None

    start_total = jnp.zeros((NBAS, NBAS), jnp.float32)
    gram, unused = lax.scan(add_block, start_total, half_ints)
    scaled = -0.5 * gram
    return scaled.reshape(N_ROWS, NBAS // N_ROWS, NBAS).transpose(1, 0, 2)
```

```python
import functools

import jax
import jax.numpy as jnp
from jax import lax
from jax.experimental import pallas as pl
from jax.experimental.pallas import tpu as pltpu
from jax.sharding import PartitionSpec as P

MESH = pl.DeviceIdType.MESH
BF = jnp.bfloat16
F32 = jnp.float32
NZ, NY = 8, 4
W = 1024
K = 1536
KH = K // 2


class Ring:
    def __init__(self, size, pos, device_at, buf, recv, send_sem, recv_sem):
        self.size, self.pos, self.buf, self.recv = size, pos, buf, recv
        self.peers = (device_at(lax.rem(pos + 1, size)), device_at(lax.rem(pos + size - 1, size)))
        self.send_sem, self.recv_sem = send_sem, recv_sem
        self.m, self.rows, self.lanes = buf.shape[2:]

    def where(self, direction, i):
        distance = self.size // 2 - (i + 1) // 2
        half = (i + direction) % 2
        chunk = lax.rem(self.pos + (distance if direction == 0 else self.size - distance), self.size)
        return chunk, half

    def copy(self, direction, i):
        chunk, half = self.where(direction, i)
        return pltpu.make_async_remote_copy(
            src_ref=self.buf.at[chunk, half],
            dst_ref=self.recv.at[direction, i],
            send_sem=self.send_sem.at[direction, i],
            recv_sem=self.recv_sem.at[direction, i],
            device_id=self.peers[direction],
            device_id_type=MESH,
        )

    def step(self, i):
        for direction in range(2):
            if i >= 2:
                self.copy(direction, i - 2).wait_recv()
                chunk, half = self.where(direction, i)
                self.add(chunk, half, direction, i - 2)
            self.copy(direction, i).start()

    def add(self, chunk, half, direction, i):
        rows = min(self.rows, 32 if self.lanes == W else 128)
        parts = self.rows // rows

        def body(t, _):
            a, b = t // parts, pl.multiple_of((t % parts) * rows, rows)
            at = (chunk, half, a, pl.ds(b, rows))
            total = self.buf[at].astype(F32) + self.recv[direction, i, a, pl.ds(b, rows)].astype(F32)
            self.buf[at] = total.astype(self.buf.dtype)
            return _

        lax.fori_loop(0, self.m * parts, body, 0)

    def finish(self, put):
        last = self.size - 2
        for direction in range(2):
            self.copy(direction, last - 1).wait_recv()
            self.copy(direction, last).wait_recv()
        for half in range(2):
            up, down = (last, last - 1) if half == 0 else (last - 1, last)

            def body(t, _, half=half, up=up, down=down):
                a, side = t // 2, t % 2
                rows = self.rows // 2
                r = pl.ds(pl.multiple_of(side * rows, rows), rows)
                total = (
                    self.buf[self.pos, half, a, r].astype(F32)
                    + self.recv[0, up, a, r].astype(F32)
                    + self.recv[1, down, a, r].astype(F32)
                )
                put(half * self.m + a, side, total)
                return _

            lax.fori_loop(0, self.m * 2, body, 0)

    def drain(self):
        for direction in range(2):
            for i in range(self.size - 1):
                self.copy(direction, i).wait_send()


def gram_tiles(lhs, rhs, put):
    def body(t, _):
        i, j = t // 2, t % 2
        left = lhs[:, pl.ds(pl.multiple_of(i * 256, 256), 256)]
        right = rhs[:, pl.ds(pl.multiple_of(j * 512, 512), 512)]
        tile = lax.dot_general(left, right, (((0,), (0,)), ((), ())), preferred_element_type=F32)
        put(i, j, tile.astype(BF))
        return _

    lax.fori_loop(0, 8, body, 0)


def kernel(
    x_ref, out_ref, mate_x, got, mate_got,
    dy, dz, qz, qy, e1, e2, h1, h2,
    dy_r, dz_r, qz_r, qy_r, e1_r, e2_r, h1_r, h2_r,
    ef1, ef2, ef_r, t1, t2, mix, mix_r, summed, pieces,
    dy_s, dy_t, dz_s, dz_t, qz_s, qz_t, qy_s, qy_t, e1_s, e1_t, e2_s, e2_t, h1_s, h1_t, h2_s, h2_t,
    x_s, x_t, mate_s, mate_t, ef_s, ef_t, mix_s, mix_t, piece_s, piece_t,
):
    a = lax.axis_index("aux")
    r = lax.axis_index("rows")
    z, y, l = a // 8, (a // 2) % 4, a % 2
    h, c = r // 2, r % 2
    x = 2 * h + l

    def dev(x_, y_, z_, c_):
        return (z_ * 8 + y_ * 2 + x_ % 2, 2 * (x_ // 2) + c_)

    def on_x(step):
        return dev(lax.rem(x + step, 4), y, z, c)

    mate = dev(x, y, z, 1 - c)

    barrier = pltpu.get_barrier_semaphore()
    partners = [mate] + [on_x(d) for d in (1, 2, 3)]
    partners += [dev(x, y, lax.rem(z + d, NZ), c) for d in range(1, NZ)]
    partners += [dev(x, lax.rem(y + d, NY), z, c_) for d in range(1, NY) for c_ in range(2)]
    for partner in partners:
        pl.semaphore_signal(barrier, inc=1, device_id=partner, device_id_type=MESH)
    pl.semaphore_wait(barrier, len(partners))

    def remote(src, dst, send, recv, device):
        return pltpu.make_async_remote_copy(
            src_ref=src, dst_ref=dst, send_sem=send, recv_sem=recv, device_id=device, device_id_type=MESH
        )

    def x_copy(k, step):
        target_h = lax.rem(x + step, 4) // 2
        rows = pl.ds(pl.multiple_of(target_h * KH, KH), KH)
        return remote(x_ref.at[rows], got.at[h], x_s.at[k], x_t.at[h], on_x(step))

    x_copies = [x_copy(0, 1), x_copy(1, 3)]
    for copy in x_copies:
        copy.start()
    mate_copy = remote(x_ref, mate_x, mate_s.at[0], mate_t.at[0], mate)
    mate_copy.start()

    def z_ring(*refs):
        return Ring(NZ, z, lambda p: dev(x, y, p, c), *refs)

    def y_ring(*refs):
        return Ring(NY, y, lambda p: dev(x, p, z, c), *refs)

    ring_dy = y_ring(dy, dy_r, dy_s, dy_t)
    ring_dz = z_ring(dz, dz_r, dz_s, dz_t)
    ring_e1 = z_ring(e1, e1_r, e1_s, e1_t)
    ring_e2 = y_ring(e2, e2_r, e2_s, e2_t)
    ring_qz = z_ring(qz, qz_r, qz_s, qz_t)
    ring_qy = y_ring(qy, qy_r, qy_s, qy_t)
    ring_h1 = y_ring(h1, h1_r, h1_s, h1_t)
    ring_h2 = z_ring(h2, h2_r, h2_s, h2_t)

    def put_dy(i, j, tile):
        for k in range(2):
            zi = 2 * i + k
            for yi in range(4):
                rows = tile[k * 128 + yi * 32 : k * 128 + yi * 32 + 32]
                dy[yi, zi // 4, zi % 4, :, pl.ds(pl.multiple_of(j * 512, 512), 512)] = rows

    def put_dz(i, j, tile):
        for k in range(2):
            for yi in range(4):
                rows = tile[k * 128 + yi * 32 : k * 128 + yi * 32 + 32]
                dz[2 * i + k, yi // 2, yi % 2, :, pl.ds(pl.multiple_of(j * 512, 512), 512)] = rows

    def put_qz(i, j, tile):
        for k in range(2):
            for yi in range(4):
                for n in range(4):
                    rows = tile[k * 128 + yi * 32 : k * 128 + yi * 32 + 32, n * 128 : n * 128 + 128]
                    qz[j * 4 + n, yi // 2, yi % 2, pl.ds(pl.multiple_of((2 * i + k) * 32, 32), 32), :] = rows

    def put_qy(i, j, tile):
        for k in range(2):
            for yi in range(4):
                for n in range(4):
                    rows = tile[k * 128 + yi * 32 : k * 128 + yi * 32 + 32, n * 128 : n * 128 + 128]
                    qy[yi, j, n, pl.ds(pl.multiple_of((2 * i + k) * 32, 32), 32), :] = rows

    def put_e1(n, side, total):
        e1[n, side, 0] = total

    def put_e2(n, side, total):
        e2[n, side, 0] = total

    def put_h1(n, side, total):
        h1[n, side, 0] = total

    def put_h2(n, side, total):
        h2[n, side, 0] = total

    gram_tiles(x_ref, x_ref, put_dy)
    ring_dy.step(0)
    ring_dy.step(1)
    mate_copy.wait_recv()
    gram_tiles(mate_x, x_ref, put_dz)
    ring_dz.step(0)
    ring_dz.step(1)
    ring_dy.step(2)
    for i in (2, 3, 4):
        ring_dz.step(i)
    ring_dy.finish(put_e1)
    ring_e1.step(0)
    ring_e1.step(1)
    ring_dz.step(5)
    ring_dz.step(6)
    ring_e1.step(2)
    ring_e1.step(3)
    ring_dz.finish(put_e2)
    ring_e2.step(0)
    ring_e2.step(1)

    for slot in range(2):
        remote(x_ref.at[pl.ds(0, KH)], got.at[slot], x_s.at[0], x_t.at[slot], mate).wait_recv()
    mate_got_copy = remote(got.at[0], mate_got, mate_s.at[1], mate_t.at[1], mate)
    mate_got_copy.start()
    gram_tiles(got.at[0], got.at[1], put_qz)
    ring_qz.step(0)
    ring_qz.step(1)
    mate_got_copy.wait_recv()
    gram_tiles(mate_got, got.at[1], put_qy)
    ring_qy.step(0)
    ring_qy.step(1)

    ring_e1.step(4)
    ring_e2.step(2)
    ring_e1.step(5)
    ring_e1.step(6)

    def put_ef(ref):
        def put(half, part, total):
            rows = ref.shape[1] // 2
            ref[half, pl.ds(pl.multiple_of(part * rows, rows), rows), :] = total

        return put

    ring_qz.step(2)
    ring_qz.step(3)
    ring_qy.step(2)
    ring_e1.finish(put_ef(ef1))
    ring_e2.finish(put_ef(ef2))

    near = dev(2 * h + (1 - l), y, z, c)
    ef_copies = [
        remote(ref.at[1 - l], ef_r.at[k], ef_s.at[k], ef_t.at[k], near) for k, ref in enumerate((ef1, ef2))
    ]
    for copy in ef_copies:
        copy.start()

    ring_qz.step(4)
    ring_qz.step(5)
    ring_qy.finish(put_h2)
    ring_h2.step(0)
    ring_h2.step(1)
    ring_qz.step(6)
    ring_h2.step(2)
    ring_h2.step(3)
    ring_qz.finish(put_h1)
    ring_h1.step(0)
    ring_h1.step(1)
    ring_h2.step(4)
    ring_h2.step(5)
    ring_h1.step(2)
    ring_h2.step(6)
    for k, ref in enumerate((ef1, ef2)):
        ef_copies[k].wait_recv()
        block = 2 * h + (c if k == 0 else 1 - c)
        out_ref[block] = -0.5 * (ref[l] + ef_r[k])
    ring_h1.finish(put_ef(t1))
    ring_h2.finish(put_ef(t2))

    for tile, b in ((t1, c), (t2, 1 - c)):
        for half in range(2):
            block = tile[half]
            flipped = block.T
            for n in range(4):
                for side in range(2):
                    at = n * 32 + side * 16
                    mix[2 + side, half * 4 + n, b] = block[at : at + 16]
                    mix[side, n * 2 + b, half] = flipped[at : at + 16]
    mix_copies = [
        remote(mix.at[lax.rem(x + d, 4)], mix_r.at[d - 1], mix_s.at[d - 1], mix_t.at[d - 1], on_x(d)) for d in (1, 2, 3)
    ]
    for copy in mix_copies:
        copy.start()
    for copy in mix_copies:
        copy.wait_recv()
    mine = z * h + (y * 2 + c) * (1 - h)
    for n in range(8):
        summed[n] = -0.5 * ((mix[x, n] + mix_r[0, n]) + (mix_r[1, n] + mix_r[2, n]))
    pieces[mine] = summed[mine]

    def piece_copy(d):
        n = lax.rem(mine + d, 8)
        target = dev(x, y * h + (n // 2) * (1 - h), n * h + z * (1 - h), c * h + (n % 2) * (1 - h))
        return remote(summed.at[n], pieces.at[mine], piece_s.at[d - 1], piece_t.at[d - 1], target)

    piece_copies = [piece_copy(d) for d in range(1, 8)]
    for copy in piece_copies:
        copy.start()
    for copy in piece_copies:
        copy.wait_recv()

    @pl.when(h == 1)
    def _():
        for s in range(2):
            for n in range(8):
                out_ref[s, :, n * 128 : n * 128 + 128] = pieces[n, s]

    @pl.when(h == 0)
    def _():
        for s in range(2):
            for n in range(8):
                at = (n % 4) * 32
                parts = [pieces[v * 2 + s, n // 4][:, at : at + 32] for v in range(4)]
                out_ref[2 + s, :, n * 128 : n * 128 + 128] = jnp.concatenate(parts, axis=1)

    for ring in (ring_dy, ring_dz, ring_e1, ring_e2, ring_qz, ring_qy, ring_h1, ring_h2):
        ring.drain()
    for copy in x_copies + [mate_copy, mate_got_copy] + ef_copies + mix_copies + piece_copies:
        copy.wait_send()


def shards(half_ints):
    x = jnp.pad(half_ints, ((0, 0), (0, K // 3 - half_ints.shape[1]), (0, 0))).reshape(K, W)
    dma = pltpu.SemaphoreType.DMA
    bufs = [
        ((NY, 2, 4, 32, W), BF), ((NZ, 2, 2, 32, W), BF), ((NZ, 2, 2, 256, 128), BF), ((NY, 2, 4, 256, 128), BF),
        ((NZ, 2, 1, 16, W), F32), ((NY, 2, 1, 16, W), F32), ((NY, 2, 1, 128, 128), F32), ((NZ, 2, 1, 128, 128), F32),
    ]
    recvs = [((2, shape[0] - 1) + shape[2:], dtype) for shape, dtype in bufs]
    scratch = [pltpu.VMEM((K, W), BF), pltpu.VMEM((2, KH, W), BF), pltpu.VMEM((KH, W), BF)]
    scratch += [pltpu.VMEM(shape, dtype) for shape, dtype in bufs + recvs]
    scratch += [pltpu.VMEM((2, 16, W), F32)] * 3
    scratch += [pltpu.VMEM((2, 128, 128), F32)] * 2
    scratch += [
        pltpu.VMEM((4, 8, 2, 16, 128), F32),
        pltpu.VMEM((3, 8, 2, 16, 128), F32),
        pltpu.VMEM((8, 2, 16, 128), F32),
        pltpu.VMEM((8, 2, 16, 128), F32),
    ]
    for shape, _ in bufs:
        scratch += [dma((2, shape[0] - 1))] * 2
    scratch += [dma((2,))] * 6 + [dma((3,))] * 2 + [dma((7,))] * 2
    out = pl.pallas_call(
        kernel,
        out_shape=jax.ShapeDtypeStruct((4, 16, W), F32),
        in_specs=[pl.BlockSpec(memory_space=pltpu.VMEM)],
        out_specs=pl.BlockSpec(memory_space=pltpu.VMEM),
        scratch_shapes=scratch,
        compiler_params=pltpu.CompilerParams(
            collective_id=0, has_side_effects=True, vmem_limit_bytes=56 * 1024 * 1024
        ),
        cost_estimate=pl.CostEstimate(flops=2 * 1024 * 1024 * K * 3, bytes_accessed=4 << 20, transcendentals=0),
    )(x)
    return out.transpose(1, 0, 2)


def solution(mesh):
    placed = (P("aux", None, "rows"),)
    return jax.shard_map(
        shards, mesh=mesh, in_specs=placed, out_specs=P("aux", None, "rows"), check_vma=False
    )
```

```python
import functools

import jax
import jax.numpy as jnp
from jax import lax
from jax.experimental import pallas as pl
from jax.experimental.pallas import tpu as pltpu
from jax.sharding import PartitionSpec as P

MESH = pl.DeviceIdType.MESH
BF = jnp.bfloat16
F32 = jnp.float32
NZ, NY = 8, 4
W = 1024
K = 1536
KH = K // 2
OCC = 500


class Ring:
    def __init__(self, size, pos, device_at, buf, recv, send_sem, recv_sem):
        self.size, self.pos, self.buf, self.recv = size, pos, buf, recv
        self.peers = (device_at(lax.rem(pos + 1, size)), device_at(lax.rem(pos + size - 1, size)))
        self.send_sem, self.recv_sem = send_sem, recv_sem
        self.m, self.rows, self.lanes = buf.shape[2:]

    def where(self, direction, i):
        distance = self.size // 2 - (i + 1) // 2
        half = (i + direction) % 2
        chunk = lax.rem(self.pos + (distance if direction == 0 else self.size - distance), self.size)
        return chunk, half

    def copy(self, direction, i):
        chunk, half = self.where(direction, i)
        return pltpu.make_async_remote_copy(
            src_ref=self.buf.at[chunk, half],
            dst_ref=self.recv.at[direction, i],
            send_sem=self.send_sem.at[direction, i],
            recv_sem=self.recv_sem.at[direction, i],
            device_id=self.peers[direction],
            device_id_type=MESH,
        )

    def step(self, i):
        for direction in range(2):
            if i >= 2:
                self.copy(direction, i - 2).wait_recv()
                chunk, half = self.where(direction, i)
                self.add(chunk, half, direction, i - 2)
            self.copy(direction, i).start()

    def add(self, chunk, half, direction, i):
        rows = min(self.rows, 32 if self.lanes == W else 128)
        parts = self.rows // rows

        def body(t, _):
            a, b = t // parts, pl.multiple_of((t % parts) * rows, rows)
            at = (chunk, half, a, pl.ds(b, rows))
            total = self.buf[at].astype(F32) + self.recv[direction, i, a, pl.ds(b, rows)].astype(F32)
            self.buf[at] = total.astype(self.buf.dtype)
            return _

        lax.fori_loop(0, self.m * parts, body, 0)

    def finish(self, put, sides=1):
        last = self.size - 2
        for direction in range(2):
            self.copy(direction, last - 1).wait_recv()
            self.copy(direction, last).wait_recv()
        for half in range(2):
            up, down = (last, last - 1) if half == 0 else (last - 1, last)

            def body(t, _, half=half, up=up, down=down):
                a, side = t // sides, t % sides
                rows = self.rows // sides
                r = pl.ds(pl.multiple_of(side * rows, rows), rows)
                total = (
                    self.buf[self.pos, half, a, r].astype(F32)
                    + self.recv[0, up, a, r].astype(F32)
                    + self.recv[1, down, a, r].astype(F32)
                )
                put(half * self.m + a, side, total)
                return _

            lax.fori_loop(0, self.m * sides, body, 0)

    def drain(self):
        for direction in range(2):
            for i in range(self.size - 1):
                self.copy(direction, i).wait_send()


def gram_tiles(lhs, rhs, put):
    def body(t, _):
        i, j = t // 2, t % 2
        left = lhs[:, pl.ds(pl.multiple_of(i * 256, 256), 256)]
        right = rhs[:, pl.ds(pl.multiple_of(j * 512, 512), 512)]
        tile = lax.dot_general(left, right, (((0,), (0,)), ((), ())), preferred_element_type=F32)
        put(i, j, tile)
        return _

    lax.fori_loop(0, 8, body, 0)


def kernel(
    half_ints, out_ref, raw, x_ref, mate_x, got, mate_got,
    dy, dz, qz, qy, e1, e2, h1, h2,
    dy_r, dz_r, qz_r, qy_r, e1_r, e2_r, h1_r, h2_r,
    ef1, ef2, ef_r, t1, t2, mix, mix_b, mix_r, summed, pieces, diag, diag_sum, diag_y, diag_z,
    dy_s, dy_t, dz_s, dz_t, qz_s, qz_t, qy_s, qy_t, e1_s, e1_t, e2_s, e2_t, h1_s, h1_t, h2_s, h2_t,
    raw_t, x_s, x_t, mate_s, mate_t, ef_s, ef_t, mix_s, mix_t, piece_s, piece_t, dgy_s, dgy_t, dgz_s, dgz_t,
):
    raw_copies = [pltpu.make_async_copy(half_ints.at[p], raw.at[p], raw_t.at[p]) for p in range(3)]
    for copy in raw_copies:
        copy.start()
    a = lax.axis_index("aux")
    r = lax.axis_index("rows")
    z, y, l = a // 8, (a // 2) % 4, a % 2
    h, c = r // 2, r % 2
    x = 2 * h + l

    def dev(x_, y_, z_, c_):
        return (z_ * 8 + y_ * 2 + x_ % 2, 2 * (x_ // 2) + c_)

    def on_x(step):
        return dev(lax.rem(x + step, 4), y, z, c)

    mate = dev(x, y, z, 1 - c)

    barrier = pltpu.get_barrier_semaphore()
    partners = [mate, on_x(1), on_x(3)]
    partners += [dev(x, y, lax.rem(z + d, NZ), c) for d in (1, NZ - 1)]
    partners += [dev(x, lax.rem(y + d, NY), z, c) for d in (1, NY - 1)]
    for partner in partners:
        pl.semaphore_signal(barrier, inc=1, device_id=partner, device_id_type=MESH)
    whole = OCC // 16 * 16
    for p in range(3):
        raw_copies[p].wait()

        def body(t, _, p=p):
            rows = pl.multiple_of(t * 16, 16)
            x_ref[pl.ds(p * 512 + rows, 16), :] = raw[p, pl.ds(rows, 16), :]
            return _

        lax.fori_loop(0, whole // 16, body, 0)
        tail = jnp.zeros((512 - OCC, W), BF)
        x_ref[p * 512 + whole : p * 512 + 512, :] = jnp.concatenate([raw[p, whole:OCC, :], tail], axis=0)
    pl.semaphore_wait(barrier, len(partners))

    def remote(src, dst, send, recv, device):
        return pltpu.make_async_remote_copy(
            src_ref=src, dst_ref=dst, send_sem=send, recv_sem=recv, device_id=device, device_id_type=MESH
        )

    def x_copy(k, step):
        target_h = lax.rem(x + step, 4) // 2
        rows = pl.ds(pl.multiple_of(target_h * KH, KH), KH)
        return remote(x_ref.at[rows], got.at[h], x_s.at[k], x_t.at[h], on_x(step))

    x_copies = [x_copy(0, 1), x_copy(1, 3)]
    for copy in x_copies:
        copy.start()
    mate_copy = remote(x_ref, mate_x, mate_s.at[0], mate_t.at[0], mate)
    mate_copy.start()

    def z_ring(*refs):
        return Ring(NZ, z, lambda p: dev(x, y, p, c), *refs)

    def y_ring(*refs):
        return Ring(NY, y, lambda p: dev(x, p, z, c), *refs)

    ring_dy = y_ring(dy, dy_r, dy_s, dy_t)
    ring_dz = z_ring(dz, dz_r, dz_s, dz_t)
    ring_e1 = z_ring(e1, e1_r, e1_s, e1_t)
    ring_e2 = y_ring(e2, e2_r, e2_s, e2_t)
    ring_qz = z_ring(qz, qz_r, qz_s, qz_t)
    ring_qy = y_ring(qy, qy_r, qy_s, qy_t)
    ring_h1 = y_ring(h1, h1_r, h1_s, h1_t)
    ring_h2 = z_ring(h2, h2_r, h2_s, h2_t)

    def put_dy(i, j, tile):
        on_diagonal = lax.broadcasted_iota(jnp.int32, (256, 512), 1) - lax.broadcasted_iota(jnp.int32, (256, 512), 0)
        on_diagonal = on_diagonal == i * 256 - j * 512
        columns = pl.ds(pl.multiple_of(j * 512, 512), 512)
        diag[:, columns] += jnp.sum(jnp.where(on_diagonal, tile, 0.0), axis=0, keepdims=True)
        tile = jnp.where(on_diagonal, 0.0, tile).astype(BF)
        for k in range(2):
            zi = 2 * i + k
            for yi in range(4):
                rows = tile[k * 128 + yi * 32 : k * 128 + yi * 32 + 32]
                dy[yi, zi // 4, zi % 4, :, pl.ds(pl.multiple_of(j * 512, 512), 512)] = rows

    def put_dz(i, j, tile):
        tile = tile.astype(BF)
        for k in range(2):
            for yi in range(4):
                rows = tile[k * 128 + yi * 32 : k * 128 + yi * 32 + 32]
                dz[2 * i + k, yi // 2, yi % 2, :, pl.ds(pl.multiple_of(j * 512, 512), 512)] = rows

    def put_qz(i, j, tile):
        tile = tile.astype(BF)
        for k in range(2):
            for yi in range(4):
                for n in range(4):
                    rows = tile[k * 128 + yi * 32 : k * 128 + yi * 32 + 32, n * 128 : n * 128 + 128]
                    qz[j * 4 + n, yi // 2, yi % 2, pl.ds(pl.multiple_of((2 * i + k) * 32, 32), 32), :] = rows

    def put_qy(i, j, tile):
        tile = tile.astype(BF)
        for k in range(2):
            for yi in range(4):
                for n in range(4):
                    rows = tile[k * 128 + yi * 32 : k * 128 + yi * 32 + 32, n * 128 : n * 128 + 128]
                    qy[yi, j, n, pl.ds(pl.multiple_of((2 * i + k) * 32, 32), 32), :] = rows

    def put_e1(n, side, total):
        e1[n, side, 0] = total.astype(BF)

    def put_e2(n, side, total):
        e2[n, side, 0] = total.astype(BF)

    def put_h1(n, side, total):
        h1[n, side, 0] = total.astype(BF)

    def put_h2(n, side, total):
        h2[n, side, 0] = total.astype(BF)

    diag[...] = jnp.zeros_like(diag)
    gram_tiles(x_ref, x_ref, put_dy)
    ring_dy.step(0)
    ring_dy.step(1)
    mate_copy.wait_recv()
    gram_tiles(mate_x, x_ref, put_dz)
    ring_dz.step(0)
    ring_dz.step(1)
    ring_dy.step(2)
    for i in (2, 3, 4):
        ring_dz.step(i)
    ring_dy.finish(put_e1, 2)
    dgy_copies = [
        remote(diag, diag_y.at[d - 1], dgy_s.at[d - 1], dgy_t.at[d - 1], dev(x, lax.rem(y + d, NY), z, c))
        for d in range(1, NY)
    ]
    for copy in dgy_copies:
        copy.start()
    ring_e1.step(0)
    ring_e1.step(1)
    ring_dz.step(5)
    ring_dz.step(6)
    ring_e1.step(2)
    ring_e1.step(3)
    ring_dz.finish(put_e2, 2)
    for copy in dgy_copies:
        copy.wait_recv()
    diag_sum[...] = (diag[...] + diag_y[0]) + (diag_y[1] + diag_y[2])
    dgz_copies = [
        remote(diag_sum, diag_z.at[d - 1], dgz_s.at[d - 1], dgz_t.at[d - 1], dev(x, y, lax.rem(z + d, NZ), c))
        for d in range(1, NZ)
    ]
    for copy in dgz_copies:
        copy.start()
    ring_e2.step(0)
    ring_e2.step(1)

    for slot in range(2):
        remote(x_ref.at[pl.ds(0, KH)], got.at[slot], x_s.at[0], x_t.at[slot], mate).wait_recv()
    mate_got_copy = remote(got.at[0], mate_got, mate_s.at[1], mate_t.at[1], mate)
    mate_got_copy.start()
    gram_tiles(got.at[0], got.at[1], put_qz)
    ring_qz.step(0)
    ring_qz.step(1)
    mate_got_copy.wait_recv()
    gram_tiles(mate_got, got.at[1], put_qy)
    ring_qy.step(0)
    ring_qy.step(1)

    ring_e1.step(4)
    ring_e2.step(2)
    ring_e1.step(5)
    ring_e1.step(6)

    def put_ef(ref):
        def put(half, part, total):
            ref[half] = total

        return put

    ring_qz.step(2)
    ring_qz.step(3)
    ring_qy.step(2)
    ring_e1.finish(put_ef(ef1))
    for copy in dgz_copies:
        copy.wait_recv()
    total_diag = diag_sum[...]
    for d in range(NZ - 1):
        total_diag = total_diag + diag_z[d]
    for side in range(2):
        row = lax.broadcasted_iota(jnp.int32, (16, W), 0) + (z * 128 + y * 32 + side * 16)
        own = lax.broadcasted_iota(jnp.int32, (16, W), 1) == row
        ef1[side] += jnp.where(own, total_diag, 0.0)
    ring_e2.finish(put_ef(ef2))

    near = dev(2 * h + (1 - l), y, z, c)
    ef_copies = [
        remote(ref.at[1 - l], ef_r.at[k], ef_s.at[k], ef_t.at[k], near) for k, ref in enumerate((ef1, ef2))
    ]
    for copy in ef_copies:
        copy.start()

    ring_qz.step(4)
    ring_qz.step(5)
    ring_qy.finish(put_h2, 2)
    ring_h2.step(0)
    ring_h2.step(1)
    ring_qz.step(6)
    ring_h2.step(2)
    ring_h2.step(3)
    ring_qz.finish(put_h1, 2)
    ring_h1.step(0)
    ring_h1.step(1)
    ring_h2.step(4)
    ring_h2.step(5)
    ring_h1.step(2)
    for k, ref in enumerate((ef1, ef2)):
        ef_copies[k].wait_recv()
        block = 2 * h + (c if k == 0 else 1 - c)
        out_ref[block] = -0.5 * (ref[l] + ef_r[k])

    def mix_start(k, tile):
        for half in range(2):
            block = tile[half]
            flipped = block.T
            for n in range(4):
                for side in range(2):
                    at = n * 32 + side * 16
                    mix[k, 2 + side, half * 4 + n] = block[at : at + 16]
                    mix[k, side, n * 2 + half] = flipped[at : at + 16]
        mix_b[k] = mix[k].astype(BF)
        copies = []
        for d in (1, 2, 3):
            sems = mix_s.at[k, d - 1], mix_t.at[k, d - 1]
            copies.append(remote(mix_b.at[k, lax.rem(x + d, 4)], mix_r.at[k, d - 1], *sems, on_x(d)))
            copies[-1].start()
        return copies

    def mix_finish(k, copies):
        b = c if k == 0 else 1 - c
        for copy in copies:
            copy.wait_recv()
        for n in range(8):
            total = mix[k, x, n] + mix_r[k, 0, n].astype(F32)
            total = total + (mix_r[k, 1, n].astype(F32) + mix_r[k, 2, n].astype(F32))
            summed[n * h + (n // 2 * 2 + b) * (1 - h), b * h + n % 2 * (1 - h)] = -0.5 * total

    ring_h1.finish(put_ef(t1))
    mix_copies = mix_start(0, t1)
    ring_h2.step(6)
    ring_h2.finish(put_ef(t2))
    mix_2 = mix_start(1, t2)
    mix_finish(0, mix_copies)
    mix_finish(1, mix_2)
    mix_copies += mix_2
    mine = z * h + (y * 2 + c) * (1 - h)
    pieces[mine] = summed[mine]

    def piece_copy(d):
        n = lax.rem(mine + d, 8)
        target = dev(x, y * h + (n // 2) * (1 - h), n * h + z * (1 - h), c * h + (n % 2) * (1 - h))
        return remote(summed.at[n], pieces.at[mine], piece_s.at[d - 1], piece_t.at[d - 1], target)

    piece_copies = [piece_copy(d) for d in range(1, 8)]
    for copy in piece_copies:
        copy.start()
    for copy in piece_copies:
        copy.wait_recv()

    @pl.when(h == 1)
    def _():
        for s in range(2):
            for n in range(8):
                out_ref[s, :, n * 128 : n * 128 + 128] = pieces[n, s]

    @pl.when(h == 0)
    def _():
        for s in range(2):
            for n in range(8):
                at = (n % 4) * 32
                parts = [pieces[v * 2 + s, n // 4][:, at : at + 32] for v in range(4)]
                out_ref[2 + s, :, n * 128 : n * 128 + 128] = jnp.concatenate(parts, axis=1)

    for ring in (ring_dy, ring_dz, ring_e1, ring_e2, ring_qz, ring_qy, ring_h1, ring_h2):
        ring.drain()
    for copy in x_copies + [mate_copy, mate_got_copy] + ef_copies + mix_copies + piece_copies + dgy_copies + dgz_copies:
        copy.wait_send()


def shards(half_ints):
    dma = pltpu.SemaphoreType.DMA
    bufs = [
        ((NY, 2, 4, 32, W), BF), ((NZ, 2, 2, 32, W), BF), ((NZ, 2, 2, 256, 128), BF), ((NY, 2, 4, 256, 128), BF),
        ((NZ, 2, 1, 16, W), BF), ((NY, 2, 1, 16, W), BF), ((NY, 2, 1, 128, 128), BF), ((NZ, 2, 1, 128, 128), BF),
    ]
    recvs = [((2, shape[0] - 1) + shape[2:], dtype) for shape, dtype in bufs]
    scratch = [pltpu.VMEM((3, OCC, W), BF), pltpu.VMEM((K, W), BF)]
    scratch += [pltpu.VMEM((K, W), BF), pltpu.VMEM((2, KH, W), BF), pltpu.VMEM((KH, W), BF)]
    scratch += [pltpu.VMEM(shape, dtype) for shape, dtype in bufs + recvs]
    scratch += [pltpu.VMEM((2, 16, W), F32)] * 3
    scratch += [pltpu.VMEM((2, 128, 128), F32)] * 2
    scratch += [
        pltpu.VMEM((2, 4, 8, 16, 128), F32),
        pltpu.VMEM((2, 4, 8, 16, 128), BF),
        pltpu.VMEM((2, 3, 8, 16, 128), BF),
        pltpu.VMEM((8, 2, 16, 128), F32),
        pltpu.VMEM((8, 2, 16, 128), F32),
        pltpu.VMEM((1, W), F32),
        pltpu.VMEM((1, W), F32),
        pltpu.VMEM((NY - 1, 1, W), F32),
        pltpu.VMEM((NZ - 1, 1, W), F32),
    ]
    for shape, _ in bufs:
        scratch += [dma((2, shape[0] - 1))] * 2
    scratch += [dma((3,))] + [dma((2,))] * 6 + [dma((2, 3))] * 2 + [dma((7,))] * 2
    scratch += [dma((NY - 1,))] * 2 + [dma((NZ - 1,))] * 2
    out = pl.pallas_call(
        kernel,
        out_shape=jax.ShapeDtypeStruct((4, 16, W), F32),
        in_specs=[pl.BlockSpec(memory_space=pl.ANY)],
        out_specs=pl.BlockSpec(memory_space=pltpu.VMEM),
        scratch_shapes=scratch,
        compiler_params=pltpu.CompilerParams(
            collective_id=0, has_side_effects=True, vmem_limit_bytes=56 * 1024 * 1024
        ),
        cost_estimate=pl.CostEstimate(flops=2 * 1024 * 1024 * K * 3, bytes_accessed=4 << 20, transcendentals=0),
    )(half_ints)
    return out.transpose(1, 0, 2)


def solution(mesh):
    placed = (P("aux", None, "rows"),)
    return jax.shard_map(
        shards, mesh=mesh, in_specs=placed, out_specs=P("aux", None, "rows"), check_vma=False
    )
```

```python
import functools

import jax
import jax.numpy as jnp
from jax import lax
from jax.experimental import pallas as pl
from jax.experimental.pallas import tpu as pltpu
from jax.sharding import PartitionSpec as P

MESH = pl.DeviceIdType.MESH
BF = jnp.bfloat16
F32 = jnp.float32
NZ, NY = 8, 4
W = 1024
K = 1536
KH = K // 2
ORDER = (4, 3, 5, 2, 6, 1, 7, 0)
PARTS = 4
OCC = 500


class Ring:
    def __init__(self, size, pos, device_at, buf, recv, send_sem, recv_sem):
        self.size, self.pos, self.buf, self.recv = size, pos, buf, recv
        self.peers = (device_at(lax.rem(pos + 1, size)), device_at(lax.rem(pos + size - 1, size)))
        self.send_sem, self.recv_sem = send_sem, recv_sem
        self.m, self.rows, self.lanes = buf.shape[2:]

    def where(self, direction, i):
        distance = self.size // 2 - (i + 1) // 2
        half = (i + direction) % 2
        chunk = lax.rem(self.pos + (distance if direction == 0 else self.size - distance), self.size)
        return chunk, half

    def copy(self, direction, i):
        chunk, half = self.where(direction, i)
        return pltpu.make_async_remote_copy(
            src_ref=self.buf.at[chunk, half],
            dst_ref=self.recv.at[direction, i],
            send_sem=self.send_sem.at[direction, i],
            recv_sem=self.recv_sem.at[direction, i],
            device_id=self.peers[direction],
            device_id_type=MESH,
        )

    def step(self, i):
        for direction in range(2):
            if i >= 2:
                self.copy(direction, i - 2).wait_recv()
                chunk, half = self.where(direction, i)
                self.add(chunk, half, direction, i - 2)
            self.copy(direction, i).start()

    def add(self, chunk, half, direction, i):
        rows = min(self.rows, 32 if self.lanes == W else 128)
        parts = self.rows // rows

        def body(t, _):
            a, b = t // parts, pl.multiple_of((t % parts) * rows, rows)
            at = (chunk, half, a, pl.ds(b, rows))
            total = self.buf[at].astype(F32) + self.recv[direction, i, a, pl.ds(b, rows)].astype(F32)
            self.buf[at] = total.astype(self.buf.dtype)
            return _

        lax.fori_loop(0, self.m * parts, body, 0)

    def finish(self, put, sides=1):
        last = self.size - 2
        for direction in range(2):
            self.copy(direction, last - 1).wait_recv()
            self.copy(direction, last).wait_recv()
        for half in range(2):
            up, down = (last, last - 1) if half == 0 else (last - 1, last)

            def body(t, _, half=half, up=up, down=down):
                a, side = t // sides, t % sides
                rows = self.rows // sides
                r = pl.ds(pl.multiple_of(side * rows, rows), rows)
                total = (
                    self.buf[self.pos, half, a, r].astype(F32)
                    + self.recv[0, up, a, r].astype(F32)
                    + self.recv[1, down, a, r].astype(F32)
                )
                put(half * self.m + a, side, total)
                return _

            lax.fori_loop(0, self.m * sides, body, 0)

    def drain(self):
        for direction in range(2):
            for i in range(self.size - 1):
                self.copy(direction, i).wait_send()


def gram_tiles(lhs, rhs, put):
    def body(t, _):
        i, j = t // 2, t % 2
        left = lhs[:, pl.ds(pl.multiple_of(i * 256, 256), 256)]
        right = rhs[:, pl.ds(pl.multiple_of(j * 512, 512), 512)]
        tile = lax.dot_general(left, right, (((0,), (0,)), ((), ())), preferred_element_type=F32)
        put(i, j, tile)
        return _

    lax.fori_loop(0, 8, body, 0)


def kernel(
    half_ints, out_ref, raw, x_ref, mate_x, got, mate_got, left,
    da, db, ea, eb, q0, q1, q2, q3,
    da_r, db_r, ea_r, eb_r, q0_r, q1_r, q2_r, q3_r,
    fa, fb, f_r, tile_y, tile_y_r, tile, mix, mix_r, summed, pieces, diag, diag_sum, diag_y, diag_z,
    da_s, da_t, db_s, db_t, ea_s, ea_t, eb_s, eb_t, q0_s, q0_t, q1_s, q1_t, q2_s, q2_t, q3_s, q3_t,
    raw_t, x_s, x_t, mate_s, mate_t, f_s, f_t, ty_s, ty_t, mix_s, mix_t, piece_s, piece_t, dgy_s, dgy_t, dgz_s, dgz_t,
):
    raw_copies = [pltpu.make_async_copy(half_ints.at[p], raw.at[p], raw_t.at[p]) for p in range(3)]
    for copy in raw_copies:
        copy.start()
    a = lax.axis_index("aux")
    r = lax.axis_index("rows")
    z, y, l = a // 8, (a // 2) % 4, a % 2
    h, c = r // 2, r % 2
    x = 2 * h + l

    def dev(x_, y_, z_, c_):
        return (z_ * 8 + y_ * 2 + x_ % 2, 2 * (x_ // 2) + c_)

    def on_x(step):
        return dev(lax.rem(x + step, 4), y, z, c)

    def on_y(step):
        return dev(x, lax.rem(y + step, NY), z, c)

    def on_z(step):
        return dev(x, y, lax.rem(z + step, NZ), c)

    mate = dev(x, y, z, 1 - c)

    barrier = pltpu.get_barrier_semaphore()
    partners = [mate, on_x(1), on_x(3), on_y(1), on_y(3), on_z(1), on_z(7)]
    for partner in partners:
        pl.semaphore_signal(barrier, inc=1, device_id=partner, device_id_type=MESH)
    whole = OCC // 16 * 16
    for p in range(3):
        raw_copies[p].wait()

        def body(t, _, p=p):
            rows = pl.multiple_of(t * 16, 16)
            x_ref[pl.ds(p * 512 + rows, 16), :] = raw[p, pl.ds(rows, 16), :]
            return _

        lax.fori_loop(0, whole // 16, body, 0)
        tail = jnp.zeros((512 - OCC, W), BF)
        x_ref[p * 512 + whole : p * 512 + 512, :] = jnp.concatenate([raw[p, whole:OCC, :], tail], axis=0)
    pl.semaphore_wait(barrier, len(partners))

    def remote(src, dst, send, recv, device):
        return pltpu.make_async_remote_copy(
            src_ref=src, dst_ref=dst, send_sem=send, recv_sem=recv, device_id=device, device_id_type=MESH
        )

    def columns_of(h_, k):
        block = h_ * lax.rem(z + ORDER[k], NZ) + (1 - h_) * k
        return pl.ds(pl.multiple_of(block * 128, 128), 128)

    def x_copy(k, n, step):
        target_h = lax.rem(x + step, 4) // 2
        rows = pl.ds(pl.multiple_of(target_h * KH, KH), KH)
        columns = columns_of(h, k)
        return remote(x_ref.at[rows, columns], got.at[h, :, columns], x_s.at[n, k], x_t.at[h, k], on_x(step))

    def x_wait(slot, *ks):
        for k in ks:
            columns = columns_of(slot, k)
            remote(x_ref.at[pl.ds(0, KH), columns], got.at[slot, :, columns], x_s.at[0, k], x_t.at[slot, k], mate).wait_recv()

    x_copies = [x_copy(k, n, step) for k in range(NZ) for n, step in enumerate((1, 3))]
    for copy in x_copies:
        copy.start()
    mate_copy = remote(x_ref, mate_x, mate_s.at[PARTS], mate_t.at[PARTS], mate)
    mate_copy.start()

    def z_ring(*refs):
        return Ring(NZ, z, lambda p: dev(x, y, p, c), *refs)

    def y_ring(*refs):
        return Ring(NY, y, lambda p: dev(x, p, z, c), *refs)

    ring_a = y_ring(da, da_r, da_s, da_t)
    ring_b = y_ring(db, db_r, db_s, db_t)
    ring_ea = z_ring(ea, ea_r, ea_s, ea_t)
    ring_eb = z_ring(eb, eb_r, eb_s, eb_t)
    rings = [
        z_ring(q0, q0_r, q0_s, q0_t),
        z_ring(q1, q1_r, q1_s, q1_t),
        z_ring(q2, q2_r, q2_s, q2_t),
        z_ring(q3, q3_r, q3_s, q3_t),
    ]

    def put_rows(ref, i, j, tile_):
        tile_ = tile_.astype(BF)
        for k in range(2):
            zi = 2 * i + k
            for yi in range(4):
                rows = tile_[k * 128 + yi * 32 : k * 128 + yi * 32 + 32]
                ref[yi, zi // 4, zi % 4, :, pl.ds(pl.multiple_of(j * 512, 512), 512)] = rows

    def put_a(i, j, tile_):
        on_diagonal = lax.broadcasted_iota(jnp.int32, (256, 512), 1) - lax.broadcasted_iota(jnp.int32, (256, 512), 0)
        on_diagonal = on_diagonal == i * 256 - j * 512
        columns = pl.ds(pl.multiple_of(j * 512, 512), 512)
        diag[:, columns] += jnp.sum(jnp.where(on_diagonal, tile_, 0.0), axis=0, keepdims=True)
        put_rows(da, i, j, jnp.where(on_diagonal, 0.0, tile_))

    def put_b(i, j, tile_):
        put_rows(db, i, j, tile_)

    def put_ea(n, side, total):
        ea[n, side, 0] = total.astype(BF)

    def put_eb(n, side, total):
        eb[n, side, 0] = total.astype(BF)

    def put_f(ref):
        def put(half, part, total):
            ref[half] = total

        return put

    def mate_part(p):
        columns = pl.ds(p * 256, 256)
        return remote(got.at[0, :, columns], mate_got.at[:, columns], mate_s.at[p], mate_t.at[p], mate)

    def turn(p, which):
        rows = (mate_got[:, p * 256 : p * 256 + 256] if which else got[0, :, p * 256 : p * 256 + 256]).T
        for yi in range(4):
            for k in range(2):
                at = which * 256 + yi * 64 + k * 32
                left[p, at : at + 32, :] = rows[k * 128 + yi * 32 : k * 128 + yi * 32 + 32]

    def cross(p, *ks):
        for k in ks:
            block = lax.rem(z + ORDER[k], NZ)
            right = got[1, :, pl.ds(pl.multiple_of(block * 128, 128), 128)]
            product = lax.dot_general(left[p], right, (((1,), (0,)), ((), ())), preferred_element_type=F32).astype(BF)
            for which in range(2):
                rings[p].buf[block, which, 0] = product[which * 256 : which * 256 + 256]

    def over_y(p):
        def put(which, yi, total):
            tile_y[p, yi, which] = total.astype(BF)

        rings[p].finish(put, 4)
        copies = []
        for d in range(1, NY):
            sems = ty_s.at[p, d - 1], ty_t.at[p, d - 1]
            copies.append(remote(tile_y.at[p, lax.rem(y + d, NY)], tile_y_r.at[p, d - 1], *sems, on_y(d)))
            copies[-1].start()
        return copies

    def over_x(p, copies):
        for copy in copies:
            copy.wait_recv()
        for which in range(2):
            total = tile_y[p, y, which].astype(F32)
            for d in range(NY - 1):
                total = total + tile_y_r[p, d, which].astype(F32)
            tile[p, c if which == 0 else 1 - c] = total
        flipped = jnp.concatenate([tile[p, 0], tile[p, 1]], axis=0).T
        for side in range(2):
            for n in range(4):
                at = (n % 2) * 32 + side * 16
                mix[p, 2 + side, n] = tile[p, n // 2, at : at + 16, :]
                at = n * 32 + side * 16
                mix[p, side, n] = flipped[at : at + 16]
        out = []
        for d in (1, 2, 3):
            sems = mix_s.at[p, d - 1], mix_t.at[p, d - 1]
            out.append(remote(mix.at[p, lax.rem(x + d, 4)], mix_r.at[p, d - 1], *sems, on_x(d)))
            out[-1].start()
        return out

    def collect(p, copies):
        for copy in copies:
            copy.wait_recv()
        for n in range(4):
            total = -0.5 * ((mix[p, x, n] + mix_r[p, 0, n]) + (mix_r[p, 1, n] + mix_r[p, 2, n]))

            @pl.when(h == 1)
            def _(total=total, n=n):
                summed[2 * p + n % 2, n // 2] = total

            @pl.when(h == 0)
            def _(total=total, n=n):
                at = (p % 2) * 64
                for b in range(2):
                    summed[n * 2 + b, p // 2, :, at : at + 64] = total[:, b * 64 : b * 64 + 64]

    started = [mate_copy]

    def send_part(p):
        copy = mate_part(p)
        copy.start()
        started.append(copy)
        return copy

    diag[...] = jnp.zeros_like(diag)
    gram_tiles(x_ref, x_ref, put_a)
    ring_a.step(0)
    ring_a.step(1)
    mate_copy.wait_recv()
    gram_tiles(mate_x, x_ref, put_b)
    x_wait(0, 0, 1)
    part = send_part(0)
    turn(0, 0)
    ring_a.step(2)
    ring_b.step(0)
    ring_b.step(1)
    x_wait(1, 0, 1, 2)
    part.wait_recv()
    turn(0, 1)
    cross(0, 0, 1, 2)
    rings[0].step(0)
    rings[0].step(1)
    x_wait(0, 2, 3)
    part = send_part(1)
    turn(1, 0)
    rings[0].step(2)
    x_wait(1, 3, 4)
    cross(0, 3, 4)
    rings[0].step(3)
    part.wait_recv()
    turn(1, 1)
    cross(1, 0, 1, 2, 3, 4)
    rings[1].step(0)
    rings[1].step(1)
    ring_a.finish(put_ea, 2)
    dgy_copies = [remote(diag, diag_y.at[d - 1], dgy_s.at[d - 1], dgy_t.at[d - 1], on_y(d)) for d in range(1, NY)]
    for copy in dgy_copies:
        copy.start()
    ring_ea.step(0)
    ring_ea.step(1)
    rings[0].step(4)
    rings[1].step(2)
    x_wait(0, 4, 5)
    part = send_part(2)
    turn(2, 0)
    ring_b.step(2)
    rings[1].step(3)
    part.wait_recv()
    turn(2, 1)
    cross(2, 0, 1, 2, 3, 4)
    rings[2].step(0)
    rings[2].step(1)
    ring_ea.step(2)
    ring_ea.step(3)
    rings[1].step(4)
    rings[2].step(2)
    x_wait(1, 5, 6)
    cross(0, 5, 6)
    rings[0].step(5)
    cross(1, 5, 6)
    rings[1].step(5)
    cross(2, 5, 6)
    rings[0].step(6)
    ring_ea.step(4)
    ring_ea.step(5)
    rings[2].step(3)
    rings[1].step(6)
    x_wait(0, 6, 7)
    part = send_part(3)
    turn(3, 0)
    x_wait(1, 7)
    cross(0, 7)
    cross(1, 7)
    cross(2, 7)
    part.wait_recv()
    turn(3, 1)
    cross(3, *range(8))
    rings[3].step(0)
    rings[3].step(1)
    rings[2].step(4)
    y0 = over_y(0)
    rings[2].step(5)
    rings[3].step(2)
    y1 = over_y(1)
    rings[3].step(3)
    rings[2].step(6)
    ring_ea.step(6)
    ring_b.finish(put_eb, 2)
    ring_eb.step(0)
    ring_eb.step(1)
    for copy in dgy_copies:
        copy.wait_recv()
    diag_sum[...] = (diag[...] + diag_y[0]) + (diag_y[1] + diag_y[2])
    dgz_copies = [remote(diag_sum, diag_z.at[d - 1], dgz_s.at[d - 1], dgz_t.at[d - 1], on_z(d)) for d in range(1, NZ)]
    for copy in dgz_copies:
        copy.start()
    rings[3].step(4)
    x0 = over_x(0, y0)
    ring_eb.step(2)
    rings[3].step(5)
    x1 = over_x(1, y1)
    y2 = over_y(2)
    ring_eb.step(3)
    ring_ea.finish(put_f(fa))
    rings[3].step(6)
    ring_eb.step(4)
    collect(0, x0)
    collect(1, x1)
    ring_eb.step(5)
    x2 = over_x(2, y2)
    y3 = over_y(3)
    ring_eb.step(6)
    collect(2, x2)
    x3 = over_x(3, y3)
    ring_eb.finish(put_f(fb))
    for copy in dgz_copies:
        copy.wait_recv()
    total_diag = diag_sum[...]
    for d in range(NZ - 1):
        total_diag = total_diag + diag_z[d]
    for side in range(2):
        row = lax.broadcasted_iota(jnp.int32, (16, W), 0) + (z * 128 + y * 32 + side * 16)
        own = lax.broadcasted_iota(jnp.int32, (16, W), 1) == row
        fa[side] += jnp.where(own, total_diag, 0.0)

    near = dev(2 * h + (1 - l), y, z, c)
    f_copies = [remote(ref.at[1 - l], f_r.at[k], f_s.at[k], f_t.at[k], near) for k, ref in enumerate((fa, fb))]
    for copy in f_copies:
        copy.start()
    collect(3, x3)

    mine = z * h + (y * 2 + c) * (1 - h)

    def piece_copy(d):
        n = lax.rem(mine + d, 8)
        target = dev(x, y * h + (n // 2) * (1 - h), n * h + z * (1 - h), c * h + (n % 2) * (1 - h))
        return remote(summed.at[n], pieces.at[mine], piece_s.at[d - 1], piece_t.at[d - 1], target)

    piece_copies = [piece_copy(d) for d in range(1, 8)]
    for copy in piece_copies:
        copy.start()
    pieces[mine] = summed[mine]
    for k, ref in enumerate((fa, fb)):
        f_copies[k].wait_recv()
        block = 2 * h + (c if k == 0 else 1 - c)
        out_ref[block] = -0.5 * (ref[l] + f_r[k])
    for copy in piece_copies:
        copy.wait_recv()

    @pl.when(h == 1)
    def _():
        for s in range(2):
            for n in range(8):
                out_ref[s, :, n * 128 : n * 128 + 128] = pieces[n, s]

    @pl.when(h == 0)
    def _():
        for s in range(2):
            for n in range(8):
                at = (n % 4) * 32
                parts = [pieces[v * 2 + s, n // 4][:, at : at + 32] for v in range(4)]
                out_ref[2 + s, :, n * 128 : n * 128 + 128] = jnp.concatenate(parts, axis=1)

    for ring in [ring_a, ring_b, ring_ea, ring_eb] + rings:
        ring.drain()
    for copy in x_copies + started + y0 + y1 + y2 + y3 + x0 + x1 + x2 + x3:
        copy.wait_send()
    for copy in f_copies + piece_copies + dgy_copies + dgz_copies:
        copy.wait_send()


def shards(half_ints):
    dma = pltpu.SemaphoreType.DMA
    vmem = pltpu.VMEM
    bufs = [(NY, 2, 4, 32, W)] * 2 + [(NZ, 2, 1, 16, W)] * 2 + [(NZ, 2, 1, 256, 128)] * PARTS
    scratch = [vmem((3, OCC, W), BF), vmem((K, W), BF), vmem((K, W), BF)]
    scratch += [vmem((2, KH, W), BF), vmem((KH, W), BF), vmem((PARTS, 512, KH), BF)]
    scratch += [vmem(shape, BF) for shape in bufs]
    scratch += [vmem((2, shape[0] - 1) + shape[2:], BF) for shape in bufs]
    scratch += [vmem((2, 16, W), F32)] * 3
    scratch += [
        vmem((PARTS, NY, 2, 64, 128), BF),
        vmem((PARTS, NY - 1, 2, 64, 128), BF),
        vmem((PARTS, 2, 64, 128), F32),
        vmem((PARTS, 4, 4, 16, 128), F32),
        vmem((PARTS, 3, 4, 16, 128), F32),
        vmem((8, 2, 16, 128), F32),
        vmem((8, 2, 16, 128), F32),
        vmem((1, W), F32),
        vmem((1, W), F32),
        vmem((NY - 1, 1, W), F32),
        vmem((NZ - 1, 1, W), F32),
    ]
    for shape in bufs:
        scratch += [dma((2, shape[0] - 1))] * 2
    scratch += [dma((3,))] + [dma((2, NZ))] * 2 + [dma((PARTS + 1,))] * 2 + [dma((2,))] * 2
    scratch += [dma((PARTS, NY - 1))] * 2 + [dma((PARTS, 3))] * 2 + [dma((7,))] * 2
    scratch += [dma((NY - 1,))] * 2 + [dma((NZ - 1,))] * 2
    out = pl.pallas_call(
        kernel,
        out_shape=jax.ShapeDtypeStruct((4, 16, W), F32),
        in_specs=[pl.BlockSpec(memory_space=pl.ANY)],
        out_specs=pl.BlockSpec(memory_space=pltpu.VMEM),
        scratch_shapes=scratch,
        compiler_params=pltpu.CompilerParams(
            collective_id=0, has_side_effects=True, vmem_limit_bytes=56 * 1024 * 1024
        ),
        cost_estimate=pl.CostEstimate(flops=2 * 1024 * 1024 * K * 3, bytes_accessed=4 << 20, transcendentals=0),
    )(half_ints)
    return out.transpose(1, 0, 2)


def solution(mesh):
    placed = (P("aux", None, "rows"),)
    return jax.shard_map(
        shards, mesh=mesh, in_specs=placed, out_specs=P("aux", None, "rows"), check_vma=False
    )
```

```python
import functools

import jax
import jax.numpy as jnp
from jax import lax
from jax.experimental import pallas as pl
from jax.experimental.pallas import tpu as pltpu
from jax.sharding import PartitionSpec as P

MESH = pl.DeviceIdType.MESH
BF = jnp.bfloat16
F32 = jnp.float32
NZ, NY = 8, 4
W = 1024
K = 1536
KH = K // 2
ORDER = (4, 3, 5, 2, 6, 1, 7, 0)
PARTS = 4
SPLIT = 5
GROUPS = ((7,), (5, 6), (3, 4), (1, 2), (0,))
SCHEDULE = (
    "gC", "gA", "A.0", "A.1", "C.0", "C.1", "gB0", "gB1", "sp0", "A.2", "tu0.0", "C.2", "C.3", "B.0", "B.1", "tu0.1",
    "cr0.3", "cr0.4", "R0.0", "R0.1", "C.4", "Af", "C.5", "sp1", "tu1.0", "R0.2", "tu1.1", "C.6", "cr0.2", "R0.3",
    "ca1", "V1.0", "B.2", "V1.1", "R0.4", "Cf", "fcs", "sp2", "tu2.0", "tu2.1", "cr2.4", "R2.0", "cr2.3", "R2.1",
    "cr2.2", "V1.2", "sp3", "cr0.1", "R0.5", "tu3.0", "cr2.1", "R0.6", "tu3.1", "cr3.1", "cr3.4", "R3.0", "R2.2",
    "cr3.3", "R3.1", "cr3.2", "R2.3", "cr0.0", "sp4", "cb1", "W1.0", "W1.1", "Bf", "Ex", "tu4.0", "Y0", "tu4.1",
    "cr2.0", "R3.2", "c4.0", "c4.1", "Q.0", "dgy", "R2.4", "Q.1", "cr3.0", "R3.3", "V1f", "R1.0", "R1.1", "R2.5",
    "W1.2", "R3.4", "R2.6", "X0", "R1.2", "R3.5", "R1.3", "Q.2", "dgz", "R3.6", "W1f", "Ea", "R1.4", "E.0", "Y2",
    "Qf", "R1.5", "E.1", "K0", "G", "Y3", "R1.6", "E.2", "X2", "X3", "E.3", "Y1", "X1", "E.4", "K2", "E.5", "K3",
    "E.6", "K1", "pieces", "Ef", "out",
)
FROM = (0, 256, 512, 768, 896, 1024)
OCC = 500


class Ring:
    def __init__(self, size, pos, device_at, buf, recv, send_sem, recv_sem):
        self.size, self.pos, self.buf, self.recv = size, pos, buf, recv
        self.peers = (device_at(lax.rem(pos + 1, size)), device_at(lax.rem(pos + size - 1, size)))
        self.send_sem, self.recv_sem = send_sem, recv_sem
        self.m, self.rows, self.lanes = buf.shape[2:]

    def where(self, direction, i):
        distance = self.size // 2 - (i + 1) // 2
        half = (i + direction) % 2
        chunk = lax.rem(self.pos + (distance if direction == 0 else self.size - distance), self.size)
        return chunk, half

    def copy(self, direction, i):
        chunk, half = self.where(direction, i)
        return pltpu.make_async_remote_copy(
            src_ref=self.buf.at[chunk, half],
            dst_ref=self.recv.at[direction, i],
            send_sem=self.send_sem.at[direction, i],
            recv_sem=self.recv_sem.at[direction, i],
            device_id=self.peers[direction],
            device_id_type=MESH,
        )

    def step(self, i):
        for direction in range(2):
            if i >= 2:
                self.copy(direction, i - 2).wait_recv()
                chunk, half = self.where(direction, i)
                self.add(chunk, half, direction, i - 2)
            self.copy(direction, i).start()

    def add(self, chunk, half, direction, i):
        rows = min(self.rows, 32 if self.lanes == W else 128)
        parts = self.rows // rows

        def body(t, _):
            a, b = t // parts, pl.multiple_of((t % parts) * rows, rows)
            at = (chunk, half, a, pl.ds(b, rows))
            total = self.buf[at].astype(F32) + self.recv[direction, i, a, pl.ds(b, rows)].astype(F32)
            self.buf[at] = total.astype(self.buf.dtype)
            return _

        lax.fori_loop(0, self.m * parts, body, 0)

    def finish(self, put, sides=1):
        last = self.size - 2
        for direction in range(2):
            self.copy(direction, last - 1).wait_recv()
            self.copy(direction, last).wait_recv()
        for half in range(2):
            up, down = (last, last - 1) if half == 0 else (last - 1, last)

            def body(t, _, half=half, up=up, down=down):
                a, side = t // sides, t % sides
                rows = self.rows // sides
                r = pl.ds(pl.multiple_of(side * rows, rows), rows)
                total = (
                    self.buf[self.pos, half, a, r].astype(F32)
                    + self.recv[0, up, a, r].astype(F32)
                    + self.recv[1, down, a, r].astype(F32)
                )
                put(half * self.m + a, side, total)
                return _

            lax.fori_loop(0, self.m * sides, body, 0)

    def drain(self):
        for direction in range(2):
            for i in range(self.size - 1):
                self.copy(direction, i).wait_send()


def gram_tiles(lhs, rhs, j, put):
    def body(i, _):
        left = lhs[:, pl.ds(pl.multiple_of(i * 256, 256), 256)]
        right = rhs[:, j * 512 : j * 512 + 512]
        tile = lax.dot_general(left, right, (((0,), (0,)), ((), ())), preferred_element_type=F32)
        put(i, tile)
        return _

    lax.fori_loop(0, 4, body, 0)


def kernel(
    half_ints, out_ref, raw, x_ref, mate_x, got, mate_got, left, left_4,
    da, db, dc, e, q0, q1, q2, q3, q4, v1, w1,
    da_r, db_r, dc_r, e_r, q0_r, q1_r, q2_r, q3_r, q4_r, v1_r, w1_r,
    e_own, e_near, e_sum, fc, fc_r, gc, gc_r, h4, h4_r,
    tile_y, tile_y_r, tile, mix, mix_r, summed, pieces, diag, diag_sum, diag_y, diag_z, diag_x,
    da_s, da_t, db_s, db_t, dc_s, dc_t, e_s, e_t, q0_s, q0_t, q1_s, q1_t, q2_s, q2_t, q3_s, q3_t, q4_s, q4_t, v1_s, v1_t, w1_s, w1_t,
    raw_t, x_s, x_t, mate_s, mate_t, near_s, near_t, ty_s, ty_t, mix_s, mix_t, piece_s, piece_t,
    dgy_s, dgy_t, dgz_s, dgz_t, fc_s, fc_t, h4_s, h4_t,
):
    raw_copies = [pltpu.make_async_copy(half_ints.at[p], raw.at[p], raw_t.at[p]) for p in range(3)]
    for copy in raw_copies:
        copy.start()
    a = lax.axis_index("aux")
    r = lax.axis_index("rows")
    z, y, l = a // 8, (a // 2) % 4, a % 2
    h, c = r // 2, r % 2
    x = 2 * h + l

    def dev(x_, y_, z_, c_):
        return (z_ * 8 + y_ * 2 + x_ % 2, 2 * (x_ // 2) + c_)

    def on_x(step):
        return dev(lax.rem(x + step, 4), y, z, c)

    def on_y(step):
        return dev(x, lax.rem(y + step, NY), z, c)

    def on_z(step):
        return dev(x, y, lax.rem(z + step, NZ), c)

    mate = dev(x, y, z, 1 - c)

    barrier = pltpu.get_barrier_semaphore()
    partners = [mate, on_x(1), on_x(3), on_y(1), on_y(3), on_z(1), on_z(7)]
    for partner in partners:
        pl.semaphore_signal(barrier, inc=1, device_id=partner, device_id_type=MESH)
    whole = OCC // 16 * 16
    for p in range(3):
        raw_copies[p].wait()

        def body(t, _, p=p):
            rows = pl.multiple_of(t * 16, 16)
            x_ref[pl.ds(p * 512 + rows, 16), :] = raw[p, pl.ds(rows, 16), :]
            return _

        lax.fori_loop(0, whole // 16, body, 0)
        tail = jnp.zeros((512 - OCC, W), BF)
        x_ref[p * 512 + whole : p * 512 + 512, :] = jnp.concatenate([raw[p, whole:OCC, :], tail], axis=0)
    pl.semaphore_wait(barrier, len(partners))

    def remote(src, dst, send, recv, device):
        return pltpu.make_async_remote_copy(
            src_ref=src, dst_ref=dst, send_sem=send, recv_sem=recv, device_id=device, device_id_type=MESH
        )

    def columns_of(h_, k):
        block = h_ * lax.rem(z + ORDER[k], NZ) + (1 - h_) * k
        return pl.ds(pl.multiple_of(block * 128, 128), 128)

    def x_copy(k, n, step):
        target_h = lax.rem(x + step, 4) // 2
        rows = pl.ds(pl.multiple_of(target_h * KH, KH), KH)
        columns = columns_of(h, k)
        return remote(x_ref.at[rows, columns], got.at[h, :, columns], x_s.at[n, k], x_t.at[h, k], on_x(step))

    arrived = set()

    def x_wait(slot, *ks):
        for k in ks:
            if (slot, k) in arrived:
                continue
            arrived.add((slot, k))
            columns = columns_of(slot, k)
            remote(x_ref.at[pl.ds(0, KH), columns], got.at[slot, :, columns], x_s.at[0, k], x_t.at[slot, k], mate).wait_recv()

    x_copies = [x_copy(k, n, step) for k in range(NZ) for n, step in enumerate((1, 3))]
    for copy in x_copies:
        copy.start()
    mate_copy = remote(x_ref, mate_x, mate_s.at[5], mate_t.at[5], mate)
    mate_copy.start()

    def z_ring(*refs):
        return Ring(NZ, z, lambda p: dev(x, y, p, c), *refs)

    def y_ring(*refs):
        return Ring(NY, y, lambda p: dev(x, p, z, c), *refs)

    ring_a = y_ring(da, da_r, da_s, da_t)
    ring_b = y_ring(db, db_r, db_s, db_t)
    ring_c = z_ring(dc, dc_r, dc_s, dc_t)
    ring_e = z_ring(e, e_r, e_s, e_t)
    rings = [
        z_ring(q0, q0_r, q0_s, q0_t),
        z_ring(q1, q1_r, q1_s, q1_t),
        z_ring(q2, q2_r, q2_s, q2_t),
        z_ring(q3, q3_r, q3_s, q3_t),
    ]
    ring_4 = y_ring(q4, q4_r, q4_s, q4_t)
    ring_v = y_ring(v1, v1_r, v1_s, v1_t)
    ring_w = y_ring(w1, w1_r, w1_s, w1_t)

    def no_diagonal(i, j, tile_):
        on_diagonal = lax.broadcasted_iota(jnp.int32, (256, 512), 1) - lax.broadcasted_iota(jnp.int32, (256, 512), 0)
        on_diagonal = on_diagonal == i * 256 - j * 512
        diag[:, j * 512 : j * 512 + 512] += jnp.sum(jnp.where(on_diagonal, tile_, 0.0), axis=0, keepdims=True)
        return jnp.where(on_diagonal, 0.0, tile_)

    def put_y(ref, columns, i, tile_):
        tile_ = tile_.astype(BF)
        for k in range(2):
            zi = 2 * i + k
            for yi in range(4):
                rows = tile_[k * 128 + yi * 32 : k * 128 + yi * 32 + 32]
                ref[yi, zi // 4, zi % 4, :, columns] = rows

    def put_a(i, tile_):
        put_y(da, slice(0, 512), i, no_diagonal(i, 1, tile_))

    def put_c(i, tile_):
        tile_ = no_diagonal(i, 0, tile_).astype(BF)
        for k in range(2):
            for yi in range(4):
                dc[2 * i + k, yi // 2, yi % 2] = tile_[k * 128 + yi * 32 : k * 128 + yi * 32 + 32]

    def put_ea(n, side, total):
        e_own[side, n, 0, :, 0:512] = total.astype(BF)

    def put_eb(n, side, total):
        e_own[side, n, 0, :, 512:768] = total[:, 0:256].astype(BF)
        e_own[side, n, 1] = total[:, 256:1024].astype(BF)

    def put_fc(n, side, total):
        fc[n] = total.astype(BF)

    def put_e(half, part, total):
        e_sum[half] = total

    def mate_part(p):
        columns = pl.ds(FROM[p], FROM[p + 1] - FROM[p])
        return remote(got.at[0, :, columns], mate_got.at[:, columns], mate_s.at[p], mate_t.at[p], mate)

    def turn(p, which):
        size = FROM[p + 1] - FROM[p]
        ref = left.at[p] if p < 3 else left_4.at[p - 3]
        columns = slice(FROM[p], FROM[p + 1])
        rows = (mate_got[:, columns] if which else got[0, :, columns]).T
        for yi in range(4):
            for k in range(size // 128):
                at = which * size + yi * (size // 4) + k * 32
                ref[at : at + 32, :] = rows[k * 128 + yi * 32 : k * 128 + yi * 32 + 32]

    def cross(p, *ks):
        size = FROM[p + 1] - FROM[p]
        for k in ks:
            block = lax.rem(z + ORDER[k], NZ)
            right = got[1, :, pl.ds(pl.multiple_of(block * 128, 128), 128)]
            rows = left[p] if p < 3 else left_4[p - 3]
            product = lax.dot_general(rows, right, (((1,), (0,)), ((), ())), preferred_element_type=F32).astype(BF)
            for which in range(2):
                if p != 1:
                    rings[p].buf[block, which, 0] = product[which * size : which * size + size]
                    continue
                ref, n = (v1, k) if k < SPLIT else (w1, k - SPLIT)
                for yi in range(4):
                    at = which * size + yi * 64
                    ref[yi, which, n] = product[at : at + 64]

    def cross_4(which):
        rows = left_4[1, which * 128 : which * 128 + 128]
        for j in range(4):
            right = got[1, :, j * 256 : j * 256 + 256]
            product = lax.dot_general(rows, right, (((1,), (0,)), ((), ())), preferred_element_type=F32).astype(BF)
            for yi in range(4):
                for n in range(2):
                    q4[yi, which, 2 * j + n] = product[yi * 32 : yi * 32 + 32, n * 128 : n * 128 + 128]

    def put_q1(first, count):
        def put(n, side, total):
            k = first + n % count
            ahead = 0
            for i, step in enumerate(ORDER):
                ahead = ahead + step * jnp.where(k == i, 1, 0)
            q1[lax.rem(z + ahead, NZ), n // count, 0] = total.astype(BF)

        return put

    def put_tile_1(which, side, total):
        tile[1, c * (1 - which) + (1 - c) * which] = total

    def put_h4(n, side, total):
        h4[n % 8, n // 8] = total.astype(BF)

    def direct(src, dst, send, recv, size, pos, step_to):
        copies = []
        for d in range(1, size):
            copies.append(
                remote(src.at[lax.rem(pos + d, size)], dst.at[d - 1], send.at[d - 1], recv.at[d - 1], step_to(d))
            )
            copies[-1].start()
        return copies

    def over_y(p):
        def put(which, yi, total):
            if p < 3:
                tile_y[p, yi, which] = total.astype(BF)
            else:
                tile_y[p, yi, which, 0:32] = total.astype(BF)

        rings[p].finish(put, 4)
        rows = slice(0, 64 if p < 3 else 32)
        return direct(tile_y.at[p, :, :, rows], tile_y_r.at[p, :, :, rows], ty_s.at[p], ty_t.at[p], NY, y, on_y)

    def over_x(p, copies):
        for copy in copies:
            copy.wait_recv()
        rows = slice(0, 64 if p < 3 else 32)
        for which in range(2 if p != 1 else 0):
            total = tile_y[p, y, which, rows].astype(F32)
            for d in range(NY - 1):
                total = total + tile_y_r[p, d, which, rows].astype(F32)
            tile[p, c if which == 0 else 1 - c, rows] = total
        if p == 3:
            received("h4")
            for which in range(2):
                total = h4[z, which].astype(F32)
                for d in range(NZ - 1):
                    total = total + h4_r[d, which].astype(F32)
                tile[p, c if which == 0 else 1 - c, 32:64] = total
        flipped = jnp.concatenate([tile[p, 0], tile[p, 1]], axis=0).T
        for side in range(2):
            for n in range(4):
                at = (n % 2) * 32 + side * 16
                mix[p, 2 + side, n] = tile[p, n // 2, at : at + 16, :]
                at = n * 32 + side * 16
                mix[p, side, n] = flipped[at : at + 16]
        out = []
        for d in (1, 2, 3):
            sems = mix_s.at[p, d - 1], mix_t.at[p, d - 1]
            out.append(remote(mix.at[p, lax.rem(x + d, 4)], mix_r.at[p, d - 1], *sems, on_x(d)))
            out[-1].start()
        return out

    def collect(p, copies):
        for copy in copies:
            copy.wait_recv()
        for n in range(4):
            total = -0.5 * ((mix[p, x, n] + mix_r[p, 0, n]) + (mix_r[p, 1, n] + mix_r[p, 2, n]))

            @pl.when(h == 1)
            def _(total=total, n=n):
                summed[2 * p + n % 2, n // 2] = total

            @pl.when(h == 0)
            def _(total=total, n=n):
                at = (p % 2) * 64
                for b in range(2):
                    summed[n * 2 + b, p // 2, :, at : at + 64] = total[:, b * 64 : b * 64 + 64]

    ring_of = {
        "A": ring_a, "B": ring_b, "C": ring_c, "E": ring_e, "Q": ring_4, "V1": ring_v, "W1": ring_w,
        "R0": rings[0], "R1": rings[1], "R2": rings[2], "R3": rings[3],
    }
    sent = {}
    task = {}
    near = dev(2 * h + (1 - l), y, z, c)
    mine = z * h + (y * 2 + c) * (1 - h)

    def do(f):
        task[f.__name__.rstrip("_")] = f
        return f

    def received(name):
        for copy in sent[name]:
            copy.wait_recv()

    def start(name, *copies):
        sent[name] = copies
        for copy in copies:
            copy.start()

    @do
    def gC():
        diag[...] = jnp.zeros_like(diag)
        gram_tiles(x_ref, x_ref, 0, put_c)

    @do
    def gA():
        gram_tiles(x_ref, x_ref, 1, put_a)

    @do
    def gB0():
        mate_copy.wait_recv()
        gram_tiles(mate_x, x_ref, 0, lambda i, tile_: put_y(db, slice(0, 512), i, tile_))

    @do
    def gB1():
        gram_tiles(mate_x, x_ref, 1, lambda i, tile_: put_y(db, slice(512, 1024), i, tile_))

    @do
    def dgy():
        start("dgy", *[remote(diag, diag_y.at[d - 1], dgy_s.at[d - 1], dgy_t.at[d - 1], on_y(d)) for d in range(1, NY)])

    @do
    def dgz():
        received("dgy")
        diag_sum[...] = (diag[...] + diag_y[0]) + (diag_y[1] + diag_y[2])
        start(
            "dgz",
            *[remote(diag_sum, diag_z.at[d - 1], dgz_s.at[d - 1], dgz_t.at[d - 1], on_z(d)) for d in range(1, NZ)],
        )

    @do
    def fcs():
        sent["fc"] = direct(fc, fc_r, fc_s, fc_t, NY, y, on_y)

    @do
    def Ex():
        start("Ex", remote(e_own.at[1 - l], e_near, near_s.at[0], near_t.at[0], near))

    @do
    def Ea():
        received("Ex")

        def add_near(t, _):
            n, half = t // 2, t % 2
            total = e_own[l, n, half].astype(F32) + e_near[n, half].astype(F32)
            e[n, half, 0] = total.astype(BF)
            return _

        lax.fori_loop(0, 16, add_near, 0)

    @do
    def G():
        received("fc")
        total = fc[y].astype(F32)
        for d in range(NY - 1):
            total = total + fc_r[d].astype(F32)
        gc[0] = total[0:16]
        gc[1] = total[16:32]
        received("dgz")
        total = diag_sum[...]
        for d in range(NZ - 1):
            total = total + diag_z[d]
        diag_x[0] = total
        start(
            "G",
            remote(gc.at[1 - l], gc_r, near_s.at[1], near_t.at[1], near),
            remote(diag_x.at[0], diag_x.at[1], near_s.at[2], near_t.at[2], near),
        )

    @do
    def Ef():
        received("G")
        ring_e.finish(put_e)
        row = lax.broadcasted_iota(jnp.int32, (16, W), 0) + (z * 128 + y * 32 + l * 16)
        on_diagonal = lax.broadcasted_iota(jnp.int32, (16, W), 1) == row
        total = jnp.concatenate([gc[l] + gc_r[...], e_sum[0, :, 0:512]], axis=1)
        out_ref[2 * h + c] = -0.5 * (total + jnp.where(on_diagonal, diag_x[0] + diag_x[1], 0.0))
        out_ref[2 * h + 1 - c] = -0.5 * jnp.concatenate([e_sum[0, :, 512:768], e_sum[1]], axis=1)

    @do
    def pieces_():
        def piece_copy(d):
            n = lax.rem(mine + d, 8)
            target = dev(x, y * h + (n // 2) * (1 - h), n * h + z * (1 - h), c * h + (n % 2) * (1 - h))
            return remote(summed.at[n], pieces.at[mine], piece_s.at[d - 1], piece_t.at[d - 1], target)

        start("pieces", *[piece_copy(d) for d in range(1, 8)])
        pieces[mine] = summed[mine]

    @do
    def out():
        received("pieces")

        @pl.when(h == 1)
        def _():
            for s in range(2):
                for n in range(8):
                    out_ref[s, :, n * 128 : n * 128 + 128] = pieces[n, s]

        @pl.when(h == 0)
        def _():
            for s in range(2):
                for n in range(8):
                    at = (n % 4) * 32
                    parts = [pieces[v * 2 + s, n // 4][:, at : at + 32] for v in range(4)]
                    out_ref[2 + s, :, n * 128 : n * 128 + 128] = jnp.concatenate(parts, axis=1)

    task["Af"] = lambda: ring_a.finish(put_ea, 2)
    task["Bf"] = lambda: ring_b.finish(put_eb, 2)
    task["Cf"] = lambda: ring_c.finish(put_fc)
    task["V1f"] = lambda: ring_v.finish(put_q1(0, SPLIT))
    task["W1f"] = lambda: ring_w.finish(put_q1(SPLIT, NZ - SPLIT))
    task["Y1"] = lambda: rings[1].finish(put_tile_1)

    for name, ring in ring_of.items():
        for i in range(ring.size - 1):
            task[f"{name}.{i}"] = functools.partial(ring.step, i)

    def part_tasks(p):
        def send():
            x_wait(0, *range(FROM[p] // 128, FROM[p + 1] // 128))
            start(f"mp{p}", mate_part(p))

        def turn_mate():
            received(f"mp{p}")
            turn(p, 1)

        def cross_group(ks):
            x_wait(1, *ks)
            cross(p, *ks)

        def sum_y():
            sent[f"Y{p}"] = over_y(p)

        def sum_x():
            sent[f"X{p}"] = over_x(p, sent[f"Y{p}"] if p != 1 else ())

        task[f"sp{p}"] = send
        task[f"tu{p}.0"] = lambda: turn(p, 0)
        task[f"tu{p}.1"] = turn_mate
        if p == 4:
            return
        for d, ks in enumerate(GROUPS):
            task[f"cr{p}.{d}"] = functools.partial(cross_group, ks)
        if p != 1:
            task[f"Y{p}"] = sum_y
        task[f"X{p}"] = sum_x
        task[f"K{p}"] = lambda: collect(p, sent[f"X{p}"])
        if p == 1:
            task["ca1"] = lambda: cross_group(tuple(range(SPLIT)))
            task["cb1"] = lambda: cross_group(tuple(range(SPLIT, NZ)))

    for p in range(5):
        part_tasks(p)

    def last_part(which):
        x_wait(1, *range(NZ))
        cross_4(which)

    task["c4.0"] = lambda: last_part(0)
    task["c4.1"] = lambda: last_part(1)

    @do
    def Qf():
        ring_4.finish(put_h4)
        sent["h4"] = direct(h4, h4_r, h4_s, h4_t, NZ, z, on_z)

    for name in SCHEDULE:
        task[name]()
    for ring in ring_of.values():
        ring.drain()
    for copy in x_copies + [mate_copy]:
        copy.wait_send()
    for copies in sent.values():
        for copy in copies:
            copy.wait_send()


def shards(half_ints):
    dma = pltpu.SemaphoreType.DMA
    vmem = pltpu.VMEM
    bufs = [(NY, 2, 4, 32, 512), (NY, 2, 4, 32, W), (NZ, 2, 2, 32, 512), (NZ, 2, 1, 16, 768)]
    bufs += [(NZ, 2, 1, 256, 128), (NZ, 2, 1, 64, 128), (NZ, 2, 1, 256, 128), (NZ, 2, 1, 128, 128)]
    bufs += [(NY, 2, 8, 32, 128), (NY, 2, SPLIT, 64, 128), (NY, 2, NZ - SPLIT, 64, 128)]
    scratch = [vmem((3, OCC, W), BF), vmem((K, W), BF), vmem((K, W), BF)]
    scratch += [vmem((2, KH, W), BF), vmem((KH, W), BF), vmem((3, 512, KH), BF), vmem((2, 256, KH), BF)]
    scratch += [vmem(shape, BF) for shape in bufs]
    scratch += [vmem((2, shape[0] - 1) + shape[2:], BF) for shape in bufs]
    scratch += [
        vmem((2, NZ, 2, 16, 768), BF),
        vmem((NZ, 2, 16, 768), BF),
        vmem((2, 16, 768), F32),
        vmem((NY, 32, 512), BF),
        vmem((NY - 1, 32, 512), BF),
        vmem((2, 16, 512), F32),
        vmem((16, 512), F32),
        vmem((NZ, 2, 32, 128), BF),
        vmem((NZ - 1, 2, 32, 128), BF),
        vmem((PARTS, NY, 2, 64, 128), BF),
        vmem((PARTS, NY - 1, 2, 64, 128), BF),
        vmem((PARTS, 2, 64, 128), F32),
        vmem((PARTS, 4, 4, 16, 128), F32),
        vmem((PARTS, 3, 4, 16, 128), F32),
        vmem((8, 2, 16, 128), F32),
        vmem((8, 2, 16, 128), F32),
        vmem((1, W), F32),
        vmem((1, W), F32),
        vmem((NY - 1, 1, W), F32),
        vmem((NZ - 1, 1, W), F32),
        vmem((2, 1, W), F32),
    ]
    for shape in bufs:
        scratch += [dma((2, shape[0] - 1))] * 2
    scratch += [dma((3,))] + [dma((2, NZ))] * 2 + [dma((6,))] * 2 + [dma((3,))] * 2
    scratch += [dma((PARTS, NY - 1))] * 2 + [dma((PARTS, 3))] * 2 + [dma((7,))] * 2
    scratch += [dma((NY - 1,))] * 2 + [dma((NZ - 1,))] * 2 + [dma((NY - 1,))] * 2 + [dma((NZ - 1,))] * 2
    out = pl.pallas_call(
        kernel,
        out_shape=jax.ShapeDtypeStruct((4, 16, W), F32),
        in_specs=[pl.BlockSpec(memory_space=pl.ANY)],
        out_specs=pl.BlockSpec(memory_space=pltpu.VMEM),
        scratch_shapes=scratch,
        compiler_params=pltpu.CompilerParams(
            collective_id=0, has_side_effects=True, vmem_limit_bytes=56 * 1024 * 1024
        ),
        cost_estimate=pl.CostEstimate(flops=2 * 1024 * 1024 * K * 3, bytes_accessed=4 << 20, transcendentals=0),
    )(half_ints)
    return out.transpose(1, 0, 2)


def solution(mesh):
    placed = (P("aux", None, "rows"),)
    return jax.shard_map(
        shards, mesh=mesh, in_specs=placed, out_specs=P("aux", None, "rows"), check_vma=False
    )
```

```python
import functools

import jax
import jax.numpy as jnp
from jax import lax
from jax.experimental import pallas as pl
from jax.experimental.pallas import tpu as pltpu
from jax.sharding import PartitionSpec as P

MESH = pl.DeviceIdType.MESH
BF = jnp.bfloat16
F32 = jnp.float32
NZ, NY = 8, 4
W = 1024
K = 1536
KH = K // 2
ORDER = (4, 3, 5, 2, 6, 1, 7, 0)
PARTS = 4
SPLITS = (0, 5, 7, 8)
EARLY = 2
CZ, CW = 768, 768
CA, EH = W - CZ, W - CZ // 2
GROUPS = ((7,), (5, 6), (3, 4), (1, 2), (0,))
SCHEDULE = (
    "gC0", "C0.0", "gA", "A.0", "A.1", "C0.1", "gB0", "C0.2", "gB1", "A.2", "sp0", "B.0", "B.1", "tu0.0", "C0.3",
    "C0.4", "tu0.1", "cr0.3", "cr0.4", "R0.0", "R0.1", "Af", "C0.5", "sp1", "tu1.0", "C0.6", "R0.2", "tu1.1", "cr1.4",
    "R1.0", "cr1.3", "B.2", "R1.1", "cr0.2", "R0.3", "cr1.2", "Cf", "fcs", "sp2", "tu2.0", "R0.4", "R1.2", "tu2.1",
    "cV2", "V2.0", "V2.1", "R1.3", "sp3", "cr0.1", "cr1.1", "R0.5", "Bf", "dgy", "cU2", "R0.6", "tu3.0", "U2.0",
    "U2.1", "tu3.1", "cr3.2", "cr3.1", "cr3.3", "cr3.4", "R3.0", "R3.1", "R1.4", "R1.5", "Ex", "cr1.0", "cW2", "V2.2",
    "cr3.0", "W2.0", "W2.1", "sp4", "cr0.0", "tu4.0", "c4.0", "dgz", "Y0", "tu4.1", "c4.1", "Q.0", "U2.2", "R3.2",
    "Q.1", "R3.3", "V2f", "R2.0", "R1.6", "R2.1", "W2.2", "X0", "G", "R3.4", "Q.2", "R3.5", "R2.2", "Ea", "U2f",
    "E.0", "E.1", "Y1", "R2.3", "W2f", "K0", "R3.6", "R2.4", "Qf", "E.2", "E.3", "R2.5", "X1", "Y3", "R2.6", "X3",
    "K1", "E.4", "pieces0", "E.5", "Y2", "X2", "E.6", "K3", "K2", "pieces1", "Ef", "out",
)
FROM = (0, 256, 512, 768, 896, 1024)
OCC = 500


class Ring:
    def __init__(self, size, pos, device_at, buf, recv, send_sem, recv_sem):
        self.size, self.pos, self.buf, self.recv = size, pos, buf, recv
        self.peers = (device_at(lax.rem(pos + 1, size)), device_at(lax.rem(pos + size - 1, size)))
        self.send_sem, self.recv_sem = send_sem, recv_sem
        self.m, self.rows, self.lanes = buf.shape[2:]

    def where(self, direction, i):
        distance = self.size // 2 - (i + 1) // 2
        half = (i + direction) % 2
        chunk = lax.rem(self.pos + (distance if direction == 0 else self.size - distance), self.size)
        return chunk, half

    def copy(self, direction, i):
        chunk, half = self.where(direction, i)
        return pltpu.make_async_remote_copy(
            src_ref=self.buf.at[chunk, half],
            dst_ref=self.recv.at[direction, i],
            send_sem=self.send_sem.at[direction, i],
            recv_sem=self.recv_sem.at[direction, i],
            device_id=self.peers[direction],
            device_id_type=MESH,
        )

    def step(self, i):
        for direction in range(2):
            if i >= 2:
                self.copy(direction, i - 2).wait_recv()
                chunk, half = self.where(direction, i)
                self.add(chunk, half, direction, i - 2)
            self.copy(direction, i).start()

    def add(self, chunk, half, direction, i):
        rows = min(self.rows, 32 if self.lanes == W else 128)
        parts = self.rows // rows

        def body(t, _):
            a, b = t // parts, pl.multiple_of((t % parts) * rows, rows)
            at = (chunk, half, a, pl.ds(b, rows))
            total = self.buf[at].astype(F32) + self.recv[direction, i, a, pl.ds(b, rows)].astype(F32)
            self.buf[at] = total.astype(self.buf.dtype)
            return _

        lax.fori_loop(0, self.m * parts, body, 0)

    def finish(self, put, sides=1):
        last = self.size - 2
        for direction in range(2):
            self.copy(direction, last - 1).wait_recv()
            self.copy(direction, last).wait_recv()
        for half in range(2):
            up, down = (last, last - 1) if half == 0 else (last - 1, last)

            def body(t, _, half=half, up=up, down=down):
                a, side = t // sides, t % sides
                rows = self.rows // sides
                r = pl.ds(pl.multiple_of(side * rows, rows), rows)
                total = (
                    self.buf[self.pos, half, a, r].astype(F32)
                    + self.recv[0, up, a, r].astype(F32)
                    + self.recv[1, down, a, r].astype(F32)
                )
                put(half * self.m + a, side, total)
                return _

            lax.fori_loop(0, self.m * sides, body, 0)

    def drain(self):
        for direction in range(2):
            for i in range(self.size - 1):
                self.copy(direction, i).wait_send()


def gram_tiles(lhs, rhs, first, width, put):
    def body(i, _):
        left = lhs[:, pl.ds(pl.multiple_of(i * 256, 256), 256)]
        right = rhs[:, first : first + width]
        tile = lax.dot_general(left, right, (((0,), (0,)), ((), ())), preferred_element_type=F32)
        put(i, tile)
        return _

    lax.fori_loop(0, 4, body, 0)


def kernel(
    half_ints, out_ref, raw, x_ref, mate_x, got, mate_got, left, left_4,
    da, db, dc0, e, q0, q1, q2, q3, q4, v2, u2, w2,
    da_r, db_r, dc0_r, e_r, q0_r, q1_r, q2_r, q3_r, q4_r, v2_r, u2_r, w2_r,
    e_own, e_near, e_sum, fc, fc_r, gc, gc_r, h4, h4_r,
    tile_y, tile_y_r, tile, mix, mix_r, summed, pieces, diag, diag_sum, diag_y, diag_z, diag_x,
    da_s, da_t, db_s, db_t, dc0_s, dc0_t, e_s, e_t,
    q0_s, q0_t, q1_s, q1_t, q2_s, q2_t, q3_s, q3_t, q4_s, q4_t, v2_s, v2_t, u2_s, u2_t, w2_s, w2_t,
    raw_t, x_s, x_t, mate_s, mate_t, near_s, near_t, ty_s, ty_t, mix_s, mix_t, piece_s, piece_t, piece0_s, piece0_t,
    dgy_s, dgy_t, dgz_s, dgz_t, fc_s, fc_t, h4_s, h4_t,
):
    raw_copies = [pltpu.make_async_copy(half_ints.at[p], raw.at[p], raw_t.at[p]) for p in range(3)]
    for copy in raw_copies:
        copy.start()
    a = lax.axis_index("aux")
    r = lax.axis_index("rows")
    z, y, l = a // 8, (a // 2) % 4, a % 2
    h, c = r // 2, r % 2
    x = 2 * h + l

    def dev(x_, y_, z_, c_):
        return (z_ * 8 + y_ * 2 + x_ % 2, 2 * (x_ // 2) + c_)

    def on_x(step):
        return dev(lax.rem(x + step, 4), y, z, c)

    def on_y(step):
        return dev(x, lax.rem(y + step, NY), z, c)

    def on_z(step):
        return dev(x, y, lax.rem(z + step, NZ), c)

    mate = dev(x, y, z, 1 - c)

    barrier = pltpu.get_barrier_semaphore()
    partners = [mate, on_x(1), on_x(3), on_y(1), on_y(3), on_z(1), on_z(7)]
    for partner in partners:
        pl.semaphore_signal(barrier, inc=1, device_id=partner, device_id_type=MESH)
    whole = OCC // 16 * 16
    for p in range(3):
        raw_copies[p].wait()

        def body(t, _, p=p):
            rows = pl.multiple_of(t * 16, 16)
            x_ref[pl.ds(p * 512 + rows, 16), :] = raw[p, pl.ds(rows, 16), :]
            return _

        lax.fori_loop(0, whole // 16, body, 0)
        tail = jnp.zeros((512 - OCC, W), BF)
        x_ref[p * 512 + whole : p * 512 + 512, :] = jnp.concatenate([raw[p, whole:OCC, :], tail], axis=0)
    pl.semaphore_wait(barrier, len(partners))

    def remote(src, dst, send, recv, device):
        return pltpu.make_async_remote_copy(
            src_ref=src, dst_ref=dst, send_sem=send, recv_sem=recv, device_id=device, device_id_type=MESH
        )

    def columns_of(h_, k):
        block = h_ * lax.rem(z + ORDER[k], NZ) + (1 - h_) * k
        return pl.ds(pl.multiple_of(block * 128, 128), 128)

    def x_copy(k, n, step):
        target_h = lax.rem(x + step, 4) // 2
        rows = pl.ds(pl.multiple_of(target_h * KH, KH), KH)
        columns = columns_of(h, k)
        return remote(x_ref.at[rows, columns], got.at[h, :, columns], x_s.at[n, k], x_t.at[h, k], on_x(step))

    arrived = set()

    def x_wait(slot, *ks):
        for k in ks:
            if (slot, k) in arrived:
                continue
            arrived.add((slot, k))
            columns = columns_of(slot, k)
            remote(x_ref.at[pl.ds(0, KH), columns], got.at[slot, :, columns], x_s.at[0, k], x_t.at[slot, k], mate).wait_recv()

    x_copies = [x_copy(k, n, step) for k in range(NZ) for n, step in enumerate((1, 3))]
    for copy in x_copies:
        copy.start()
    mate_copy = remote(x_ref, mate_x, mate_s.at[5], mate_t.at[5], mate)
    mate_copy.start()

    def z_ring(*refs):
        return Ring(NZ, z, lambda p: dev(x, y, p, c), *refs)

    def y_ring(*refs):
        return Ring(NY, y, lambda p: dev(x, p, z, c), *refs)

    ring_a = y_ring(da, da_r, da_s, da_t)
    ring_b = y_ring(db, db_r, db_s, db_t)
    rings_c = [
        z_ring(dc0, dc0_r, dc0_s, dc0_t),
    ]
    ring_e = z_ring(e, e_r, e_s, e_t)
    rings = [
        z_ring(q0, q0_r, q0_s, q0_t),
        z_ring(q1, q1_r, q1_s, q1_t),
        z_ring(q2, q2_r, q2_s, q2_t),
        z_ring(q3, q3_r, q3_s, q3_t),
    ]
    ring_4 = y_ring(q4, q4_r, q4_s, q4_t)
    rings_early = [y_ring(v2, v2_r, v2_s, v2_t), y_ring(u2, u2_r, u2_s, u2_t), y_ring(w2, w2_r, w2_s, w2_t)]

    def no_diagonal(i, first, tile_):
        ahead = lax.broadcasted_iota(jnp.int32, tile_.shape, 1) - lax.broadcasted_iota(jnp.int32, tile_.shape, 0)
        on_diagonal = ahead == i * 256 - first
        diag[:, first : first + tile_.shape[1]] += jnp.sum(jnp.where(on_diagonal, tile_, 0.0), axis=0, keepdims=True)
        return jnp.where(on_diagonal, 0.0, tile_)

    def put_y(ref, columns, i, tile_):
        tile_ = tile_.astype(BF)
        for k in range(2):
            zi = 2 * i + k
            for yi in range(4):
                rows = tile_[k * 128 + yi * 32 : k * 128 + yi * 32 + 32]
                ref[yi, zi // 4, zi % 4, :, columns] = rows

    def put_a(i, tile_):
        put_y(da, slice(0, CA), i, no_diagonal(i, CZ, tile_))

    def put_c(n):
        def put(i, tile_):
            tile_ = no_diagonal(i, n * CW, tile_).astype(BF)
            for k in range(2):
                for yi in range(4):
                    rings_c[n].buf[2 * i + k, yi // 2, yi % 2] = tile_[k * 128 + yi * 32 : k * 128 + yi * 32 + 32]

        return put

    def put_ea(n, side, total):
        e_own[side, n, 0, :, 0:CA] = total.astype(BF)

    def put_eb(n, side, total):
        e_own[side, n, 0, :, CA:EH] = total[:, 0 : EH - CA].astype(BF)
        e_own[side, n, 1] = total[:, EH - CA : W].astype(BF)

    def put_fc(k):
        def put(n, side, total):
            fc[n, :, k * CW : k * CW + CW] = total.astype(BF)

        return put

    def put_e(half, part, total):
        e_sum[half] = total

    def mate_part(p):
        columns = pl.ds(FROM[p], FROM[p + 1] - FROM[p])
        return remote(got.at[0, :, columns], mate_got.at[:, columns], mate_s.at[p], mate_t.at[p], mate)

    def turn(p, which):
        size = FROM[p + 1] - FROM[p]
        ref = left.at[p] if p < 3 else left_4.at[p - 3]
        columns = slice(FROM[p], FROM[p + 1])
        rows = (mate_got[:, columns] if which else got[0, :, columns]).T
        for yi in range(4):
            for k in range(size // 128):
                at = which * size + yi * (size // 4) + k * 32
                ref[at : at + 32, :] = rows[k * 128 + yi * 32 : k * 128 + yi * 32 + 32]

    def cross(p, *ks):
        size = FROM[p + 1] - FROM[p]
        for k in ks:
            block = lax.rem(z + ORDER[k], NZ)
            right = got[1, :, pl.ds(pl.multiple_of(block * 128, 128), 128)]
            rows = left[p] if p < 3 else left_4[p - 3]
            product = lax.dot_general(rows, right, (((1,), (0,)), ((), ())), preferred_element_type=F32).astype(BF)
            for which in range(2):
                if p != EARLY:
                    rings[p].buf[block, which, 0] = product[which * size : which * size + size]
                    continue
                i = max(i for i in range(3) if SPLITS[i] <= k)
                for yi in range(4):
                    at = which * size + yi * 64
                    rings_early[i].buf[yi, which, k - SPLITS[i]] = product[at : at + 64]

    def cross_4(which):
        rows = left_4[1, which * 128 : which * 128 + 128]
        for j in range(4):
            right = got[1, :, j * 256 : j * 256 + 256]
            product = lax.dot_general(rows, right, (((1,), (0,)), ((), ())), preferred_element_type=F32).astype(BF)
            for yi in range(4):
                for n in range(2):
                    q4[yi, which, 2 * j + n] = product[yi * 32 : yi * 32 + 32, n * 128 : n * 128 + 128]

    def put_early(first, count):
        def put(n, side, total):
            k = first + n % count
            ahead = 0
            for i, step in enumerate(ORDER):
                ahead = ahead + step * jnp.where(k == i, 1, 0)
            rings[EARLY].buf[lax.rem(z + ahead, NZ), n // count, 0] = total.astype(BF)

        return put

    def put_tile_early(which, side, total):
        tile[EARLY, c * (1 - which) + (1 - c) * which] = total

    def put_h4(n, side, total):
        h4[n % 8, n // 8] = total.astype(BF)

    def direct(src, dst, send, recv, size, pos, step_to):
        copies = []
        for d in range(1, size):
            copies.append(
                remote(src.at[lax.rem(pos + d, size)], dst.at[d - 1], send.at[d - 1], recv.at[d - 1], step_to(d))
            )
            copies[-1].start()
        return copies

    def over_y(p):
        def put(which, yi, total):
            if p < 3:
                tile_y[p, yi, which] = total.astype(BF)
            else:
                tile_y[p, yi, which, 0:32] = total.astype(BF)

        rings[p].finish(put, 4)
        rows = slice(0, 64 if p < 3 else 32)
        return direct(tile_y.at[p, :, :, rows], tile_y_r.at[p, :, :, rows], ty_s.at[p], ty_t.at[p], NY, y, on_y)

    def over_x(p, copies):
        for copy in copies:
            copy.wait_recv()
        rows = slice(0, 64 if p < 3 else 32)
        for which in range(2 if p != EARLY else 0):
            total = tile_y[p, y, which, rows].astype(F32)
            for d in range(NY - 1):
                total = total + tile_y_r[p, d, which, rows].astype(F32)
            tile[p, c if which == 0 else 1 - c, rows] = total
        if p == 3:
            received("h4")
            for which in range(2):
                total = h4[z, which].astype(F32)
                for d in range(NZ - 1):
                    total = total + h4_r[d, which].astype(F32)
                tile[p, c if which == 0 else 1 - c, 32:64] = total
        flipped = jnp.concatenate([tile[p, 0], tile[p, 1]], axis=0).T
        for side in range(2):
            for n in range(4):
                at = (n % 2) * 32 + side * 16
                mix[p, 2 + side, n] = tile[p, n // 2, at : at + 16, :]
                at = n * 32 + side * 16
                mix[p, side, n] = flipped[at : at + 16]
        out = []
        for d in (1, 2, 3):
            sems = mix_s.at[p, d - 1], mix_t.at[p, d - 1]
            out.append(remote(mix.at[p, lax.rem(x + d, 4)], mix_r.at[p, d - 1], *sems, on_x(d)))
            out[-1].start()
        return out

    def collect(p, copies):
        for copy in copies:
            copy.wait_recv()
        for n in range(4):
            total = -0.5 * ((mix[p, x, n] + mix_r[p, 0, n]) + (mix_r[p, 1, n] + mix_r[p, 2, n]))

            @pl.when(h == 1)
            def _(total=total, n=n):
                summed[p // 2, 4 * (p % 2) + n % 2 * 2 + n // 2] = total

            @pl.when(h == 0)
            def _(total=total, n=n):
                at = (p % 2) * 64
                for b in range(2):
                    summed[p // 2, n * 2 + b, :, at : at + 64] = total[:, b * 64 : b * 64 + 64]

    ring_of = {"A": ring_a, "B": ring_b, "E": ring_e, "Q": ring_4}
    ring_of.update({f"C{i}": ring for i, ring in enumerate(rings_c)})
    ring_of.update({f"R{i}": ring for i, ring in enumerate(rings)})
    ring_of.update({f"{i}{EARLY}": ring for i, ring in zip("VUW", rings_early)})
    sent = {}
    task = {}
    near = dev(2 * h + (1 - l), y, z, c)
    mine = y * 2 + c

    def do(f):
        task[f.__name__.rstrip("_")] = f
        return f

    def received(name):
        for copy in sent[name]:
            copy.wait_recv()

    def start(name, *copies):
        sent[name] = copies
        for copy in copies:
            copy.start()

    def gC(n):
        if n == 0:
            diag[...] = jnp.zeros_like(diag)
        gram_tiles(x_ref, x_ref, n * CW, CW, put_c(n))

    for n in range(CZ // CW):
        task[f"gC{n}"] = functools.partial(gC, n)

    @do
    def gA():
        gram_tiles(x_ref, x_ref, CZ, CA, put_a)

    @do
    def gB0():
        mate_copy.wait_recv()
        gram_tiles(mate_x, x_ref, 0, 512, lambda i, tile_: put_y(db, slice(0, 512), i, tile_))

    @do
    def gB1():
        gram_tiles(mate_x, x_ref, 512, 512, lambda i, tile_: put_y(db, slice(512, 1024), i, tile_))

    @do
    def dgy():
        start("dgy", *[remote(diag, diag_y.at[d - 1], dgy_s.at[d - 1], dgy_t.at[d - 1], on_y(d)) for d in range(1, NY)])

    @do
    def dgz():
        received("dgy")
        diag_sum[...] = (diag[...] + diag_y[0]) + (diag_y[1] + diag_y[2])
        start(
            "dgz",
            *[remote(diag_sum, diag_z.at[d - 1], dgz_s.at[d - 1], dgz_t.at[d - 1], on_z(d)) for d in range(1, NZ)],
        )

    @do
    def fcs():
        sent["fc"] = direct(fc, fc_r, fc_s, fc_t, NY, y, on_y)

    @do
    def Ex():
        start("Ex", remote(e_own.at[1 - l], e_near, near_s.at[0], near_t.at[0], near))

    @do
    def Ea():
        received("Ex")

        def add_near(t, _):
            n, half = t // 2, t % 2
            total = e_own[l, n, half].astype(F32) + e_near[n, half].astype(F32)
            e[n, half, 0] = total.astype(BF)
            return _

        lax.fori_loop(0, 16, add_near, 0)

    @do
    def G():
        received("fc")
        total = fc[y].astype(F32)
        for d in range(NY - 1):
            total = total + fc_r[d].astype(F32)
        gc[0] = total[0:16]
        gc[1] = total[16:32]
        received("dgz")
        total = diag_sum[...]
        for d in range(NZ - 1):
            total = total + diag_z[d]
        diag_x[0] = total
        start(
            "G",
            remote(gc.at[1 - l], gc_r, near_s.at[1], near_t.at[1], near),
            remote(diag_x.at[0], diag_x.at[1], near_s.at[2], near_t.at[2], near),
        )

    @do
    def Ef():
        received("G")
        ring_e.finish(put_e)
        row = lax.broadcasted_iota(jnp.int32, (16, W), 0) + (z * 128 + y * 32 + l * 16)
        on_diagonal = lax.broadcasted_iota(jnp.int32, (16, W), 1) == row
        total = jnp.concatenate([gc[l] + gc_r[...], e_sum[0, :, 0:CA]], axis=1)
        out_ref[2 * h + c] = -0.5 * (total + jnp.where(on_diagonal, diag_x[0] + diag_x[1], 0.0))
        out_ref[2 * h + 1 - c] = -0.5 * jnp.concatenate([e_sum[0, :, CA:EH], e_sum[1]], axis=1)

    def row_piece(n):
        src = summed.at[n // 4, n % 4 * 2 : n % 4 * 2 + 2]
        return remote(src, pieces.at[z], piece_s.at[n], piece_t.at[z], dev(x, y, n, c))

    def row_wait(n):
        src = summed.at[n // 4, n % 4 * 2 : n % 4 * 2 + 2]
        return remote(src, pieces.at[n], piece_s.at[n], piece_t.at[n], dev(x, y, n, c))

    def column_piece(q, d):
        n = lax.rem(mine + d, 8)
        sems = piece0_s.at[q, d - 1], piece0_t.at[q, d - 1]
        return remote(summed.at[q, n], pieces.at[mine, q], *sems, dev(x, n // 2, z, n % 2))

    def send_pieces(q):
        @pl.when(h == 1)
        def _():
            for n in range(4 * q, 4 * q + 4):

                @pl.when(n != z)
                def _(n=n):
                    row_piece(n).start()

                @pl.when(n == z)
                def _(n=n):
                    pieces[n] = summed[q, n % 4 * 2 : n % 4 * 2 + 2]

        @pl.when(h == 0)
        def _():
            for d in range(1, 8):
                column_piece(q, d).start()
            pieces[mine, q] = summed[q, mine]

    task["pieces0"] = lambda: send_pieces(0)
    task["pieces1"] = lambda: send_pieces(1)

    @do
    def out():
        @pl.when(h == 1)
        def _():
            for n in range(8):

                @pl.when(n != z)
                def _(n=n):
                    row_wait(n).wait()

            for s in range(2):
                for n in range(8):
                    out_ref[s, :, n * 128 : n * 128 + 128] = pieces[n, s]

        @pl.when(h == 0)
        def _():
            for q in range(2):
                for d in range(1, 8):
                    column_piece(q, d).wait()
            for s in range(2):
                for n in range(8):
                    at = (n % 4) * 32
                    parts = [pieces[v * 2 + s, n // 4][:, at : at + 32] for v in range(4)]
                    out_ref[2 + s, :, n * 128 : n * 128 + 128] = jnp.concatenate(parts, axis=1)

    task["Af"] = lambda: ring_a.finish(put_ea, 2)
    task["Bf"] = lambda: ring_b.finish(put_eb, 2)
    for n, letter in enumerate("VUW"):
        count = SPLITS[n + 1] - SPLITS[n]
        task[f"{letter}{EARLY}f"] = functools.partial(rings_early[n].finish, put_early(SPLITS[n], count))
    task[f"Y{EARLY}"] = lambda: rings[EARLY].finish(put_tile_early)

    @do
    def Cf():
        for n, ring in enumerate(rings_c):
            ring.finish(put_fc(n))


    for name, ring in ring_of.items():
        for i in range(ring.size - 1):
            task[f"{name}.{i}"] = functools.partial(ring.step, i)

    def part_tasks(p):
        def send():
            x_wait(0, *range(FROM[p] // 128, FROM[p + 1] // 128))
            start(f"mp{p}", mate_part(p))

        def turn_mate():
            received(f"mp{p}")
            turn(p, 1)

        def cross_group(ks):
            x_wait(1, *ks)
            cross(p, *ks)

        def sum_y():
            sent[f"Y{p}"] = over_y(p)

        def sum_x():
            sent[f"X{p}"] = over_x(p, sent[f"Y{p}"] if p != EARLY else ())

        task[f"sp{p}"] = send
        task[f"tu{p}.0"] = lambda: turn(p, 0)
        task[f"tu{p}.1"] = turn_mate
        if p == 4:
            return
        for d, ks in enumerate(GROUPS):
            task[f"cr{p}.{d}"] = functools.partial(cross_group, ks)
        if p != EARLY:
            task[f"Y{p}"] = sum_y
        task[f"X{p}"] = sum_x
        task[f"K{p}"] = lambda: collect(p, sent[f"X{p}"])
        if p == EARLY:
            for n, letter in enumerate("VUW"):
                task[f"c{letter}{EARLY}"] = functools.partial(cross_group, tuple(range(SPLITS[n], SPLITS[n + 1])))

    for p in range(5):
        part_tasks(p)

    def last_part(which):
        x_wait(1, *range(NZ))
        cross_4(which)

    task["c4.0"] = lambda: last_part(0)
    task["c4.1"] = lambda: last_part(1)

    @do
    def Qf():
        ring_4.finish(put_h4)
        sent["h4"] = direct(h4, h4_r, h4_s, h4_t, NZ, z, on_z)

    for name in SCHEDULE:
        task[name]()
    for ring in ring_of.values():
        ring.drain()
    for copy in x_copies + [mate_copy]:
        copy.wait_send()
    for copies in sent.values():
        for copy in copies:
            copy.wait_send()


def shards(half_ints):
    dma = pltpu.SemaphoreType.DMA
    vmem = pltpu.VMEM
    bufs = [(NY, 2, 4, 32, CA), (NY, 2, 4, 32, W)] + [(NZ, 2, 2, 32, CW)] * (CZ // CW) + [(NZ, 2, 1, 16, EH)]
    bufs += [(NZ, 2, 1, 64 if p == EARLY else 256, 128) for p in range(3)]
    bufs += [(NZ, 2, 1, 128, 128), (NY, 2, 8, 32, 128)]
    bufs += [(NY, 2, SPLITS[i + 1] - SPLITS[i], 64, 128) for i in range(3)]
    scratch = [vmem((3, OCC, W), BF), vmem((K, W), BF), vmem((K, W), BF)]
    scratch += [vmem((2, KH, W), BF), vmem((KH, W), BF), vmem((3, 512, KH), BF), vmem((2, 256, KH), BF)]
    scratch += [vmem(shape, BF) for shape in bufs]
    scratch += [vmem((2, shape[0] - 1) + shape[2:], BF) for shape in bufs]
    scratch += [
        vmem((2, NZ, 2, 16, EH), BF),
        vmem((NZ, 2, 16, EH), BF),
        vmem((2, 16, EH), F32),
        vmem((NY, 32, CZ), BF),
        vmem((NY - 1, 32, CZ), BF),
        vmem((2, 16, CZ), F32),
        vmem((16, CZ), F32),
        vmem((NZ, 2, 32, 128), BF),
        vmem((NZ - 1, 2, 32, 128), BF),
        vmem((PARTS, NY, 2, 64, 128), BF),
        vmem((PARTS, NY - 1, 2, 64, 128), BF),
        vmem((PARTS, 2, 64, 128), F32),
        vmem((PARTS, 4, 4, 16, 128), F32),
        vmem((PARTS, 3, 4, 16, 128), F32),
        vmem((2, 8, 16, 128), F32),
        vmem((8, 2, 16, 128), F32),
        vmem((1, W), F32),
        vmem((1, W), F32),
        vmem((NY - 1, 1, W), F32),
        vmem((NZ - 1, 1, W), F32),
        vmem((2, 1, W), F32),
    ]
    for shape in bufs:
        scratch += [dma((2, shape[0] - 1))] * 2
    scratch += [dma((3,))] + [dma((2, NZ))] * 2 + [dma((6,))] * 2 + [dma((3,))] * 2
    scratch += [dma((PARTS, NY - 1))] * 2 + [dma((PARTS, 3))] * 2 + [dma((NZ,))] * 2 + [dma((2, 7))] * 2
    scratch += [dma((NY - 1,))] * 2 + [dma((NZ - 1,))] * 2 + [dma((NY - 1,))] * 2 + [dma((NZ - 1,))] * 2
    out = pl.pallas_call(
        kernel,
        out_shape=jax.ShapeDtypeStruct((4, 16, W), F32),
        in_specs=[pl.BlockSpec(memory_space=pl.ANY)],
        out_specs=pl.BlockSpec(memory_space=pltpu.VMEM),
        scratch_shapes=scratch,
        compiler_params=pltpu.CompilerParams(
            collective_id=0, has_side_effects=True, vmem_limit_bytes=56 * 1024 * 1024
        ),
        cost_estimate=pl.CostEstimate(flops=2 * 1024 * 1024 * K * 3, bytes_accessed=4 << 20, transcendentals=0),
    )(half_ints)
    return out.transpose(1, 0, 2)


def solution(mesh):
    placed = (P("aux", None, "rows"),)
    return jax.shard_map(
        shards, mesh=mesh, in_specs=placed, out_specs=P("aux", None, "rows"), check_vma=False
    )
```

```python
import functools

import jax
import jax.numpy as jnp
from jax import lax
from jax.experimental import pallas as pl
from jax.experimental.pallas import tpu as pltpu
from jax.sharding import PartitionSpec as P

MESH = pl.DeviceIdType.MESH
BF = jnp.bfloat16
F32 = jnp.float32
NZ, NY = 8, 4
W = 1024
K = 1536
KH = K // 2
ORDER = (4, 3, 5, 2, 6, 1, 7, 0)
PARTS = 4
SPLITS = (0, 5, 7, 8)
EARLY = 2
CZ, CW = 768, 768
CA, EH = W - CZ, W - CZ // 2
GROUPS = ((7,), (5, 6), (3, 4), (1, 2), (0,))
SCHEDULE = (
    "gC0", "C0.0", "gA", "A.0", "A.1", "C0.1", "gB0", "C0.2", "gB1", "A.2", "sp0", "B.0", "B.1", "tu0.0", "C0.3",
    "C0.4", "tu0.1", "cr0.3", "cr0.4", "R0.0", "R0.1", "Af", "C0.5", "sp1", "tu1.0", "C0.6", "R0.2", "tu1.1", "cr1.4",
    "R1.0", "cr1.3", "B.2", "R1.1", "cr0.2", "R0.3", "cr1.2", "Cf", "fcs", "sp2", "tu2.0", "R0.4", "R1.2", "tu2.1",
    "cV2", "V2.0", "V2.1", "R1.3", "sp3", "cr0.1", "cr1.1", "R0.5", "Bf", "dgy", "cU2", "R0.6", "tu3.0", "U2.0",
    "U2.1", "tu3.1", "cr3.2", "cr3.1", "cr3.3", "cr3.4", "R3.0", "R3.1", "R1.4", "R1.5", "Ex", "cr1.0", "cW2", "V2.2",
    "cr3.0", "W2.0", "W2.1", "sp4", "cr0.0", "tu4.0", "c4.0", "dgz", "Y0", "tu4.1", "c4.1", "Q.0", "U2.2", "R3.2",
    "Q.1", "R3.3", "V2f", "R2.0", "R1.6", "R2.1", "W2.2", "X0", "G", "R3.4", "Q.2", "R3.5", "R2.2", "Ea", "U2f",
    "E.0", "E.1", "Y1", "R2.3", "W2f", "K0", "R3.6", "R2.4", "Qf", "E.2", "E.3", "R2.5", "X1", "Y3", "R2.6", "X3",
    "K1", "E.4", "pieces0", "E.5", "Y2", "X2", "E.6", "K3", "K2", "pieces1", "Ef",
)
FROM = (0, 256, 512, 768, 896, 1024)
OCC = 500


class Ring:
    def __init__(self, size, pos, device_at, buf, recv, send_sem, recv_sem):
        self.size, self.pos, self.buf, self.recv = size, pos, buf, recv
        self.peers = (device_at(lax.rem(pos + 1, size)), device_at(lax.rem(pos + size - 1, size)))
        self.send_sem, self.recv_sem = send_sem, recv_sem
        self.m, self.rows, self.lanes = buf.shape[2:]

    def where(self, direction, i):
        distance = self.size // 2 - (i + 1) // 2
        half = (i + direction) % 2
        chunk = lax.rem(self.pos + (distance if direction == 0 else self.size - distance), self.size)
        return chunk, half

    def copy(self, direction, i):
        chunk, half = self.where(direction, i)
        return pltpu.make_async_remote_copy(
            src_ref=self.buf.at[chunk, half],
            dst_ref=self.recv.at[direction, i],
            send_sem=self.send_sem.at[direction, i],
            recv_sem=self.recv_sem.at[direction, i],
            device_id=self.peers[direction],
            device_id_type=MESH,
        )

    def step(self, i):
        for direction in range(2):
            if i >= 2:
                self.copy(direction, i - 2).wait_recv()
                chunk, half = self.where(direction, i)
                self.add(chunk, half, direction, i - 2)
            self.copy(direction, i).start()

    def add(self, chunk, half, direction, i):
        rows = min(self.rows, 32 if self.lanes == W else 128)
        parts = self.rows // rows

        def body(t, _):
            a, b = t // parts, pl.multiple_of((t % parts) * rows, rows)
            at = (chunk, half, a, pl.ds(b, rows))
            total = self.buf[at].astype(F32) + self.recv[direction, i, a, pl.ds(b, rows)].astype(F32)
            self.buf[at] = total.astype(self.buf.dtype)
            return _

        lax.fori_loop(0, self.m * parts, body, 0)

    def finish(self, put, sides=1):
        last = self.size - 2
        for direction in range(2):
            self.copy(direction, last - 1).wait_recv()
            self.copy(direction, last).wait_recv()
        for half in range(2):
            up, down = (last, last - 1) if half == 0 else (last - 1, last)

            def body(t, _, half=half, up=up, down=down):
                a, side = t // sides, t % sides
                rows = self.rows // sides
                r = pl.ds(pl.multiple_of(side * rows, rows), rows)
                total = (
                    self.buf[self.pos, half, a, r].astype(F32)
                    + self.recv[0, up, a, r].astype(F32)
                    + self.recv[1, down, a, r].astype(F32)
                )
                put(half * self.m + a, side, total)
                return _

            lax.fori_loop(0, self.m * sides, body, 0)

    def drain(self):
        for direction in range(2):
            for i in range(self.size - 1):
                self.copy(direction, i).wait_send()


def gram_tiles(lhs, rhs, first, width, put):
    def body(i, _):
        left = lhs[:, pl.ds(pl.multiple_of(i * 256, 256), 256)]
        right = rhs[:, first : first + width]
        tile = lax.dot_general(left, right, (((0,), (0,)), ((), ())), preferred_element_type=F32)
        put(i, tile)
        return _

    lax.fori_loop(0, 4, body, 0)


def kernel(
    half_ints, out_ref, raw, x_ref, mate_x, got, mate_got, left, left_4,
    da, db, dc0, e, q0, q1, q2, q3, q4, v2, u2, w2,
    da_r, db_r, dc0_r, e_r, q0_r, q1_r, q2_r, q3_r, q4_r, v2_r, u2_r, w2_r,
    e_own, e_near, e_sum, fc, fc_r, gc, gc_r, h4, h4_r,
    tile_y, tile_y_r, tile, mix, mix_b, mix_r, summed, pieces, diag, diag_sum, diag_y, diag_z, diag_x,
    da_s, da_t, db_s, db_t, dc0_s, dc0_t, e_s, e_t,
    q0_s, q0_t, q1_s, q1_t, q2_s, q2_t, q3_s, q3_t, q4_s, q4_t, v2_s, v2_t, u2_s, u2_t, w2_s, w2_t,
    raw_t, x_s, x_t, mate_s, mate_t, near_s, near_t, ty_s, ty_t, mix_s, mix_t, piece_s, piece_t, piece0_s, piece0_t,
    dgy_s, dgy_t, dgz_s, dgz_t, fc_s, fc_t, h4_s, h4_t,
):
    raw_copies = [pltpu.make_async_copy(half_ints.at[p], raw.at[p], raw_t.at[p]) for p in range(3)]
    for copy in raw_copies:
        copy.start()
    a = lax.axis_index("aux")
    r = lax.axis_index("rows")
    z, y, l = a // 8, (a // 2) % 4, a % 2
    h, c = r // 2, r % 2
    x = 2 * h + l

    def dev(x_, y_, z_, c_):
        return (z_ * 8 + y_ * 2 + x_ % 2, 2 * (x_ // 2) + c_)

    def on_x(step):
        return dev(lax.rem(x + step, 4), y, z, c)

    def on_y(step):
        return dev(x, lax.rem(y + step, NY), z, c)

    def on_z(step):
        return dev(x, y, lax.rem(z + step, NZ), c)

    mate = dev(x, y, z, 1 - c)

    barrier = pltpu.get_barrier_semaphore()
    partners = [mate, on_x(1), on_x(3), on_y(1), on_y(3), on_z(1), on_z(7)]
    for partner in partners:
        pl.semaphore_signal(barrier, inc=1, device_id=partner, device_id_type=MESH)
    whole = OCC // 16 * 16
    for p in range(3):
        raw_copies[p].wait()

        def body(t, _, p=p):
            rows = pl.multiple_of(t * 16, 16)
            x_ref[pl.ds(p * 512 + rows, 16), :] = raw[p, pl.ds(rows, 16), :]
            return _

        lax.fori_loop(0, whole // 16, body, 0)
        tail = jnp.zeros((512 - OCC, W), BF)
        x_ref[p * 512 + whole : p * 512 + 512, :] = jnp.concatenate([raw[p, whole:OCC, :], tail], axis=0)
    pl.semaphore_wait(barrier, len(partners))

    def remote(src, dst, send, recv, device):
        return pltpu.make_async_remote_copy(
            src_ref=src, dst_ref=dst, send_sem=send, recv_sem=recv, device_id=device, device_id_type=MESH
        )

    def columns_of(h_, k):
        block = h_ * lax.rem(z + ORDER[k], NZ) + (1 - h_) * k
        return pl.ds(pl.multiple_of(block * 128, 128), 128)

    def x_copy(k, n, step):
        target_h = lax.rem(x + step, 4) // 2
        rows = pl.ds(pl.multiple_of(target_h * KH, KH), KH)
        columns = columns_of(h, k)
        return remote(x_ref.at[rows, columns], got.at[h, :, columns], x_s.at[n, k], x_t.at[h, k], on_x(step))

    arrived = set()

    def x_wait(slot, *ks):
        for k in ks:
            if (slot, k) in arrived:
                continue
            arrived.add((slot, k))
            columns = columns_of(slot, k)
            remote(x_ref.at[pl.ds(0, KH), columns], got.at[slot, :, columns], x_s.at[0, k], x_t.at[slot, k], mate).wait_recv()

    x_copies = [x_copy(k, n, step) for k in range(NZ) for n, step in enumerate((1, 3))]
    for copy in x_copies:
        copy.start()
    mate_copy = remote(x_ref, mate_x, mate_s.at[5], mate_t.at[5], mate)
    mate_copy.start()

    def z_ring(*refs):
        return Ring(NZ, z, lambda p: dev(x, y, p, c), *refs)

    def y_ring(*refs):
        return Ring(NY, y, lambda p: dev(x, p, z, c), *refs)

    ring_a = y_ring(da, da_r, da_s, da_t)
    ring_b = y_ring(db, db_r, db_s, db_t)
    rings_c = [
        z_ring(dc0, dc0_r, dc0_s, dc0_t),
    ]
    ring_e = z_ring(e, e_r, e_s, e_t)
    rings = [
        z_ring(q0, q0_r, q0_s, q0_t),
        z_ring(q1, q1_r, q1_s, q1_t),
        z_ring(q2, q2_r, q2_s, q2_t),
        z_ring(q3, q3_r, q3_s, q3_t),
    ]
    ring_4 = y_ring(q4, q4_r, q4_s, q4_t)
    rings_early = [y_ring(v2, v2_r, v2_s, v2_t), y_ring(u2, u2_r, u2_s, u2_t), y_ring(w2, w2_r, w2_s, w2_t)]

    def no_diagonal(i, first, tile_):
        ahead = lax.broadcasted_iota(jnp.int32, tile_.shape, 1) - lax.broadcasted_iota(jnp.int32, tile_.shape, 0)
        on_diagonal = ahead == i * 256 - first
        diag[:, first : first + tile_.shape[1]] += jnp.sum(jnp.where(on_diagonal, tile_, 0.0), axis=0, keepdims=True)
        return jnp.where(on_diagonal, 0.0, tile_)

    def put_y(ref, columns, i, tile_):
        tile_ = tile_.astype(BF)
        for k in range(2):
            zi = 2 * i + k
            for yi in range(4):
                rows = tile_[k * 128 + yi * 32 : k * 128 + yi * 32 + 32]
                ref[yi, zi // 4, zi % 4, :, columns] = rows

    def put_a(i, tile_):
        put_y(da, slice(0, CA), i, no_diagonal(i, CZ, tile_))

    def put_c(n):
        def put(i, tile_):
            tile_ = no_diagonal(i, n * CW, tile_).astype(BF)
            for k in range(2):
                for yi in range(4):
                    rings_c[n].buf[2 * i + k, yi // 2, yi % 2] = tile_[k * 128 + yi * 32 : k * 128 + yi * 32 + 32]

        return put

    def put_ea(n, side, total):
        e_own[side, n, 0, :, 0:CA] = total.astype(BF)

    def put_eb(n, side, total):
        e_own[side, n, 0, :, CA:EH] = total[:, 0 : EH - CA].astype(BF)
        e_own[side, n, 1] = total[:, EH - CA : W].astype(BF)

    def put_fc(k):
        def put(n, side, total):
            fc[n, :, k * CW : k * CW + CW] = total.astype(BF)

        return put

    def put_e(half, part, total):
        e_sum[half] = total

    def mate_part(p):
        columns = pl.ds(FROM[p], FROM[p + 1] - FROM[p])
        return remote(got.at[0, :, columns], mate_got.at[:, columns], mate_s.at[p], mate_t.at[p], mate)

    def turn(p, which):
        size = FROM[p + 1] - FROM[p]
        ref = left.at[p] if p < 3 else left_4.at[p - 3]
        columns = slice(FROM[p], FROM[p + 1])
        rows = (mate_got[:, columns] if which else got[0, :, columns]).T
        for yi in range(4):
            for k in range(size // 128):
                at = which * size + yi * (size // 4) + k * 32
                ref[at : at + 32, :] = rows[k * 128 + yi * 32 : k * 128 + yi * 32 + 32]

    def cross(p, *ks):
        size = FROM[p + 1] - FROM[p]
        for k in ks:
            block = lax.rem(z + ORDER[k], NZ)
            right = got[1, :, pl.ds(pl.multiple_of(block * 128, 128), 128)]
            rows = left[p] if p < 3 else left_4[p - 3]
            product = lax.dot_general(rows, right, (((1,), (0,)), ((), ())), preferred_element_type=F32).astype(BF)
            for which in range(2):
                if p != EARLY:
                    rings[p].buf[block, which, 0] = product[which * size : which * size + size]
                    continue
                i = max(i for i in range(3) if SPLITS[i] <= k)
                for yi in range(4):
                    at = which * size + yi * 64
                    rings_early[i].buf[yi, which, k - SPLITS[i]] = product[at : at + 64]

    def cross_4(which):
        rows = left_4[1, which * 128 : which * 128 + 128]
        for j in range(4):
            right = got[1, :, j * 256 : j * 256 + 256]
            product = lax.dot_general(rows, right, (((1,), (0,)), ((), ())), preferred_element_type=F32).astype(BF)
            for yi in range(4):
                for n in range(2):
                    q4[yi, which, 2 * j + n] = product[yi * 32 : yi * 32 + 32, n * 128 : n * 128 + 128]

    def put_early(first, count):
        def put(n, side, total):
            k = first + n % count
            ahead = 0
            for i, step in enumerate(ORDER):
                ahead = ahead + step * jnp.where(k == i, 1, 0)
            rings[EARLY].buf[lax.rem(z + ahead, NZ), n // count, 0] = total.astype(BF)

        return put

    def put_tile_early(which, side, total):
        tile[EARLY, c * (1 - which) + (1 - c) * which] = total

    def put_h4(n, side, total):
        h4[n % 8, n // 8] = total.astype(BF)

    def direct(src, dst, send, recv, size, pos, step_to):
        copies = []
        for d in range(1, size):
            copies.append(
                remote(src.at[lax.rem(pos + d, size)], dst.at[d - 1], send.at[d - 1], recv.at[d - 1], step_to(d))
            )
            copies[-1].start()
        return copies

    def over_y(p):
        def put(which, yi, total):
            if p < 3:
                tile_y[p, yi, which] = total.astype(BF)
            else:
                tile_y[p, yi, which, 0:32] = total.astype(BF)

        rings[p].finish(put, 4)
        rows = slice(0, 64 if p < 3 else 32)
        return direct(tile_y.at[p, :, :, rows], tile_y_r.at[p, :, :, rows], ty_s.at[p], ty_t.at[p], NY, y, on_y)

    def over_x(p, copies):
        for copy in copies:
            copy.wait_recv()
        rows = slice(0, 64 if p < 3 else 32)
        for which in range(2 if p != EARLY else 0):
            total = tile_y[p, y, which, rows].astype(F32)
            for d in range(NY - 1):
                total = total + tile_y_r[p, d, which, rows].astype(F32)
            tile[p, c if which == 0 else 1 - c, rows] = total
        if p == 3:
            received("h4")
            for which in range(2):
                total = h4[z, which].astype(F32)
                for d in range(NZ - 1):
                    total = total + h4_r[d, which].astype(F32)
                tile[p, c if which == 0 else 1 - c, 32:64] = total
        flipped = jnp.concatenate([tile[p, 0], tile[p, 1]], axis=0).T
        for side in range(2):
            for n in range(4):
                at = (n % 2) * 32 + side * 16
                mix[p, 2 + side, n] = tile[p, n // 2, at : at + 16, :]
                at = n * 32 + side * 16
                mix[p, side, n] = flipped[at : at + 16]
        mix_b[p] = mix[p].astype(BF)
        out = []
        for d in (1, 2, 3):
            sems = mix_s.at[p, d - 1], mix_t.at[p, d - 1]
            out.append(remote(mix_b.at[p, lax.rem(x + d, 4)], mix_r.at[p, d - 1], *sems, on_x(d)))
            out[-1].start()
        return out

    def collect(p, copies):
        for copy in copies:
            copy.wait_recv()
        for n in range(4):
            total = mix[p, x, n] + mix_r[p, 0, n].astype(F32)
            total = -0.5 * (total + (mix_r[p, 1, n].astype(F32) + mix_r[p, 2, n].astype(F32)))

            @pl.when(h == 1)
            def _(total=total, n=n):
                summed[p // 2, 4 * (p % 2) + n % 2 * 2 + n // 2] = total

            @pl.when(h == 0)
            def _(total=total, n=n):
                at = (p % 2) * 64
                for b in range(2):
                    summed[p // 2, n * 2 + b, :, at : at + 64] = total[:, b * 64 : b * 64 + 64]

    ring_of = {"A": ring_a, "B": ring_b, "E": ring_e, "Q": ring_4}
    ring_of.update({f"C{i}": ring for i, ring in enumerate(rings_c)})
    ring_of.update({f"R{i}": ring for i, ring in enumerate(rings)})
    ring_of.update({f"{i}{EARLY}": ring for i, ring in zip("VUW", rings_early)})
    sent = {}
    task = {}
    near = dev(2 * h + (1 - l), y, z, c)
    mine = y * 2 + c

    def do(f):
        task[f.__name__.rstrip("_")] = f
        return f

    def received(name):
        for copy in sent[name]:
            copy.wait_recv()

    def start(name, *copies):
        sent[name] = copies
        for copy in copies:
            copy.start()

    def gC(n):
        if n == 0:
            diag[...] = jnp.zeros_like(diag)
        gram_tiles(x_ref, x_ref, n * CW, CW, put_c(n))

    for n in range(CZ // CW):
        task[f"gC{n}"] = functools.partial(gC, n)

    @do
    def gA():
        gram_tiles(x_ref, x_ref, CZ, CA, put_a)

    @do
    def gB0():
        mate_copy.wait_recv()
        gram_tiles(mate_x, x_ref, 0, 512, lambda i, tile_: put_y(db, slice(0, 512), i, tile_))

    @do
    def gB1():
        gram_tiles(mate_x, x_ref, 512, 512, lambda i, tile_: put_y(db, slice(512, 1024), i, tile_))

    @do
    def dgy():
        start("dgy", *[remote(diag, diag_y.at[d - 1], dgy_s.at[d - 1], dgy_t.at[d - 1], on_y(d)) for d in range(1, NY)])

    @do
    def dgz():
        received("dgy")
        diag_sum[...] = (diag[...] + diag_y[0]) + (diag_y[1] + diag_y[2])
        start(
            "dgz",
            *[remote(diag_sum, diag_z.at[d - 1], dgz_s.at[d - 1], dgz_t.at[d - 1], on_z(d)) for d in range(1, NZ)],
        )

    @do
    def fcs():
        sent["fc"] = direct(fc, fc_r, fc_s, fc_t, NY, y, on_y)

    @do
    def Ex():
        start("Ex", remote(e_own.at[1 - l], e_near, near_s.at[0], near_t.at[0], near))

    @do
    def Ea():
        received("Ex")

        def add_near(t, _):
            n, half = t // 2, t % 2
            total = e_own[l, n, half].astype(F32) + e_near[n, half].astype(F32)
            e[n, half, 0] = total.astype(BF)
            return _

        lax.fori_loop(0, 16, add_near, 0)

    @do
    def G():
        received("fc")
        total = fc[y].astype(F32)
        for d in range(NY - 1):
            total = total + fc_r[d].astype(F32)
        gc[0] = total[0:16]
        gc[1] = total[16:32]
        received("dgz")
        total = diag_sum[...]
        for d in range(NZ - 1):
            total = total + diag_z[d]
        diag_x[0] = total
        start(
            "G",
            remote(gc.at[1 - l], gc_r, near_s.at[1], near_t.at[1], near),
            remote(diag_x.at[0], diag_x.at[1], near_s.at[2], near_t.at[2], near),
        )

    @do
    def Ef():
        received("G")
        ring_e.finish(put_e)
        row = lax.broadcasted_iota(jnp.int32, (16, W), 0) + (z * 128 + y * 32 + l * 16)
        on_diagonal = lax.broadcasted_iota(jnp.int32, (16, W), 1) == row
        total = jnp.concatenate([gc[l] + gc_r[...], e_sum[0, :, 0:CA]], axis=1)
        out_ref[2 * h + c] = -0.5 * (total + jnp.where(on_diagonal, diag_x[0] + diag_x[1], 0.0))
        out_ref[2 * h + 1 - c] = -0.5 * jnp.concatenate([e_sum[0, :, CA:EH], e_sum[1]], axis=1)

    def row_piece(n):
        src = summed.at[n // 4, n % 4 * 2 : n % 4 * 2 + 2]
        return remote(src, pieces.at[z], piece_s.at[n], piece_t.at[z], dev(x, y, n, c))

    def row_wait(n):
        src = summed.at[n // 4, n % 4 * 2 : n % 4 * 2 + 2]
        return remote(src, pieces.at[n], piece_s.at[n], piece_t.at[n], dev(x, y, n, c))

    def column_piece(q, d):
        n = lax.rem(mine + d, 8)
        sems = piece0_s.at[q, d - 1], piece0_t.at[q, d - 1]
        return remote(summed.at[q, n], pieces.at[mine, q], *sems, dev(x, n // 2, z, n % 2))

    def send_pieces(q):
        @pl.when(h == 1)
        def _():
            for n in range(4 * q, 4 * q + 4):

                @pl.when(n != z)
                def _(n=n):
                    row_piece(n).start()

                @pl.when(n == z)
                def _(n=n):
                    pieces[n] = summed[q, n % 4 * 2 : n % 4 * 2 + 2]

        @pl.when(h == 0)
        def _():
            for d in range(1, 8):
                column_piece(q, d).start()
            pieces[mine, q] = summed[q, mine]

    task["pieces0"] = lambda: send_pieces(0)
    task["pieces1"] = lambda: send_pieces(1)

    @do
    def out():
        @pl.when(h == 1)
        def _():
            for n in range(8):

                @pl.when(n != z)
                def _(n=n):
                    row_wait(n).wait()

            for s in range(2):
                for n in range(8):
                    out_ref[s, :, n * 128 : n * 128 + 128] = pieces[n, s]

        @pl.when(h == 0)
        def _():
            for q in range(2):
                for d in range(1, 8):
                    column_piece(q, d).wait()
                for s in range(2):
                    for n in range(4):
                        parts = [pieces[v * 2 + s, q][:, n * 32 : n * 32 + 32] for v in range(4)]
                        at = q * 512 + n * 128
                        out_ref[2 + s, :, at : at + 128] = jnp.concatenate(parts, axis=1)

    task["Af"] = lambda: ring_a.finish(put_ea, 2)
    task["Bf"] = lambda: ring_b.finish(put_eb, 2)
    for n, letter in enumerate("VUW"):
        count = SPLITS[n + 1] - SPLITS[n]
        task[f"{letter}{EARLY}f"] = functools.partial(rings_early[n].finish, put_early(SPLITS[n], count))
    task[f"Y{EARLY}"] = lambda: rings[EARLY].finish(put_tile_early)

    @do
    def Cf():
        for n, ring in enumerate(rings_c):
            ring.finish(put_fc(n))


    for name, ring in ring_of.items():
        for i in range(ring.size - 1):
            task[f"{name}.{i}"] = functools.partial(ring.step, i)

    def part_tasks(p):
        def send():
            x_wait(0, *range(FROM[p] // 128, FROM[p + 1] // 128))
            start(f"mp{p}", mate_part(p))

        def turn_mate():
            received(f"mp{p}")
            turn(p, 1)

        def cross_group(ks):
            x_wait(1, *ks)
            cross(p, *ks)

        def sum_y():
            sent[f"Y{p}"] = over_y(p)

        def sum_x():
            sent[f"X{p}"] = over_x(p, sent[f"Y{p}"] if p != EARLY else ())

        task[f"sp{p}"] = send
        task[f"tu{p}.0"] = lambda: turn(p, 0)
        task[f"tu{p}.1"] = turn_mate
        if p == 4:
            return
        for d, ks in enumerate(GROUPS):
            task[f"cr{p}.{d}"] = functools.partial(cross_group, ks)
        if p != EARLY:
            task[f"Y{p}"] = sum_y
        task[f"X{p}"] = sum_x
        task[f"K{p}"] = lambda: collect(p, sent[f"X{p}"])
        if p == EARLY:
            for n, letter in enumerate("VUW"):
                task[f"c{letter}{EARLY}"] = functools.partial(cross_group, tuple(range(SPLITS[n], SPLITS[n + 1])))

    for p in range(5):
        part_tasks(p)

    def last_part(which):
        x_wait(1, *range(NZ))
        cross_4(which)

    task["c4.0"] = lambda: last_part(0)
    task["c4.1"] = lambda: last_part(1)

    @do
    def Qf():
        ring_4.finish(put_h4)
        sent["h4"] = direct(h4, h4_r, h4_s, h4_t, NZ, z, on_z)

    for name in SCHEDULE:
        task[name]()
    for ring in ring_of.values():
        ring.drain()
    for copy in x_copies + [mate_copy]:
        copy.wait_send()
    for copies in sent.values():
        for copy in copies:
            copy.wait_send()
    out()


def shards(half_ints):
    dma = pltpu.SemaphoreType.DMA
    vmem = pltpu.VMEM
    bufs = [(NY, 2, 4, 32, CA), (NY, 2, 4, 32, W)] + [(NZ, 2, 2, 32, CW)] * (CZ // CW) + [(NZ, 2, 1, 16, EH)]
    bufs += [(NZ, 2, 1, 64 if p == EARLY else 256, 128) for p in range(3)]
    bufs += [(NZ, 2, 1, 128, 128), (NY, 2, 8, 32, 128)]
    bufs += [(NY, 2, SPLITS[i + 1] - SPLITS[i], 64, 128) for i in range(3)]
    scratch = [vmem((3, OCC, W), BF), vmem((K, W), BF), vmem((K, W), BF)]
    scratch += [vmem((2, KH, W), BF), vmem((KH, W), BF), vmem((3, 512, KH), BF), vmem((2, 256, KH), BF)]
    scratch += [vmem(shape, BF) for shape in bufs]
    scratch += [vmem((2, shape[0] - 1) + shape[2:], BF) for shape in bufs]
    scratch += [
        vmem((2, NZ, 2, 16, EH), BF),
        vmem((NZ, 2, 16, EH), BF),
        vmem((2, 16, EH), F32),
        vmem((NY, 32, CZ), BF),
        vmem((NY - 1, 32, CZ), BF),
        vmem((2, 16, CZ), F32),
        vmem((16, CZ), F32),
        vmem((NZ, 2, 32, 128), BF),
        vmem((NZ - 1, 2, 32, 128), BF),
        vmem((PARTS, NY, 2, 64, 128), BF),
        vmem((PARTS, NY - 1, 2, 64, 128), BF),
        vmem((PARTS, 2, 64, 128), F32),
        vmem((PARTS, 4, 4, 16, 128), F32),
        vmem((PARTS, 4, 4, 16, 128), BF),
        vmem((PARTS, 3, 4, 16, 128), BF),
        vmem((2, 8, 16, 128), F32),
        vmem((8, 2, 16, 128), F32),
        vmem((1, W), F32),
        vmem((1, W), F32),
        vmem((NY - 1, 1, W), F32),
        vmem((NZ - 1, 1, W), F32),
        vmem((2, 1, W), F32),
    ]
    for shape in bufs:
        scratch += [dma((2, shape[0] - 1))] * 2
    scratch += [dma((3,))] + [dma((2, NZ))] * 2 + [dma((6,))] * 2 + [dma((3,))] * 2
    scratch += [dma((PARTS, NY - 1))] * 2 + [dma((PARTS, 3))] * 2 + [dma((NZ,))] * 2 + [dma((2, 7))] * 2
    scratch += [dma((NY - 1,))] * 2 + [dma((NZ - 1,))] * 2 + [dma((NY - 1,))] * 2 + [dma((NZ - 1,))] * 2
    out = pl.pallas_call(
        kernel,
        out_shape=jax.ShapeDtypeStruct((4, 16, W), F32),
        in_specs=[pl.BlockSpec(memory_space=pl.ANY)],
        out_specs=pl.BlockSpec(memory_space=pltpu.VMEM),
        scratch_shapes=scratch,
        compiler_params=pltpu.CompilerParams(
            collective_id=0, has_side_effects=True, vmem_limit_bytes=56 * 1024 * 1024
        ),
        cost_estimate=pl.CostEstimate(flops=2 * 1024 * 1024 * K * 3, bytes_accessed=4 << 20, transcendentals=0),
    )(half_ints)
    return out.transpose(1, 0, 2)


def solution(mesh):
    placed = (P("aux", None, "rows"),)
    return jax.shard_map(
        shards, mesh=mesh, in_specs=placed, out_specs=P("aux", None, "rows"), check_vma=False
    )
```

```python
import functools

import jax
import jax.numpy as jnp
from jax import lax
from jax.experimental import pallas as pl
from jax.experimental.pallas import tpu as pltpu
from jax.sharding import PartitionSpec as P

MESH = pl.DeviceIdType.MESH
BF = jnp.bfloat16
F32 = jnp.float32
NZ, NY = 8, 4
W = 1024
K = 1536
KH = K // 2
ORDER = (4, 3, 5, 2, 6, 1, 7, 0)
PARTS = 4
SPLITS = (0, 5, 7, 8)
EARLY = 2
CZ, CW = 768, 768
CA, EH = W - CZ, W - CZ // 2
GROUPS = ((7,), (5, 6), (3, 4), (1, 2), (0,))
SCHEDULE = (
    "gC0", "C0.0", "gA", "A.0", "A.1", "C0.1", "gB0", "C0.2", "gB1", "A.2", "sp0", "B.0", "B.1", "tu0.0", "C0.3",
    "C0.4", "tu0.1", "cr0.3", "cr0.4", "R0.0", "R0.1", "Af", "C0.5", "sp1", "tu1.0", "C0.6", "R0.2", "tu1.1", "cr1.4",
    "R1.0", "cr1.3", "B.2", "R1.1", "cr0.2", "R0.3", "cr1.2", "Cf", "fcs", "sp2", "tu2.0", "R0.4", "R1.2", "tu2.1",
    "cV2", "V2.0", "V2.1", "R1.3", "sp3", "cr0.1", "cr1.1", "R0.5", "Bf", "dgy", "cU2", "R0.6", "tu3.0", "U2.0",
    "U2.1", "tu3.1", "cr3.2", "cr3.1", "cr3.3", "cr3.4", "R3.0", "R3.1", "R1.4", "R1.5", "Ex", "cr1.0", "cW2", "V2.2",
    "cr3.0", "W2.0", "W2.1", "sp4", "cr0.0", "tu4.0", "c4.0", "dgz", "Y0", "tu4.1", "c4.1", "Q.0", "U2.2", "R3.2",
    "Q.1", "R3.3", "V2f", "R2.0", "R1.6", "R2.1", "W2.2", "X0", "G", "R3.4", "Q.2", "R3.5", "R2.2", "Ea", "U2f",
    "E.0", "E.1", "Y1", "R2.3", "W2f", "K0", "R3.6", "R2.4", "Qf", "E.2", "E.3", "R2.5", "X1", "Y3", "R2.6", "X3",
    "K1", "E.4", "pieces0", "E.5", "Y2", "X2", "E.6", "K3", "K2", "pieces1", "Ef",
)
FROM = (0, 256, 512, 768, 896, 1024)
OCC = 500


class Ring:
    def __init__(self, size, pos, device_at, buf, recv, send_sem, recv_sem):
        self.size, self.pos, self.buf, self.recv = size, pos, buf, recv
        self.peers = (device_at(lax.rem(pos + 1, size)), device_at(lax.rem(pos + size - 1, size)))
        self.send_sem, self.recv_sem = send_sem, recv_sem
        self.m, self.rows, self.lanes = buf.shape[2:]

    def where(self, direction, i):
        distance = self.size // 2 - (i + 1) // 2
        half = (i + direction) % 2
        chunk = lax.rem(self.pos + (distance if direction == 0 else self.size - distance), self.size)
        return chunk, half

    def copy(self, direction, i):
        chunk, half = self.where(direction, i)
        return pltpu.make_async_remote_copy(
            src_ref=self.buf.at[chunk, half],
            dst_ref=self.recv.at[direction, i],
            send_sem=self.send_sem.at[direction, i],
            recv_sem=self.recv_sem.at[direction, i],
            device_id=self.peers[direction],
            device_id_type=MESH,
        )

    def step(self, i):
        for direction in range(2):
            if i >= 2:
                self.copy(direction, i - 2).wait_recv()
                chunk, half = self.where(direction, i)
                self.add(chunk, half, direction, i - 2)
            self.copy(direction, i).start()

    def add(self, chunk, half, direction, i):
        rows = min(self.rows, 32 if self.lanes == W else 128)
        parts = self.rows // rows

        def body(t, _):
            a, b = t // parts, pl.multiple_of((t % parts) * rows, rows)
            at = (chunk, half, a, pl.ds(b, rows))
            total = self.buf[at].astype(F32) + self.recv[direction, i, a, pl.ds(b, rows)].astype(F32)
            self.buf[at] = total.astype(self.buf.dtype)
            return _

        lax.fori_loop(0, self.m * parts, body, 0)

    def finish(self, put, sides=1):
        last = self.size - 2
        for direction in range(2):
            self.copy(direction, last - 1).wait_recv()
            self.copy(direction, last).wait_recv()
        for half in range(2):
            up, down = (last, last - 1) if half == 0 else (last - 1, last)

            def body(t, _, half=half, up=up, down=down):
                a, side = t // sides, t % sides
                rows = self.rows // sides
                r = pl.ds(pl.multiple_of(side * rows, rows), rows)
                total = (
                    self.buf[self.pos, half, a, r].astype(F32)
                    + self.recv[0, up, a, r].astype(F32)
                    + self.recv[1, down, a, r].astype(F32)
                )
                put(half * self.m + a, side, total)
                return _

            lax.fori_loop(0, self.m * sides, body, 0)

    def drain(self):
        for direction in range(2):
            for i in range(self.size - 1):
                self.copy(direction, i).wait_send()


def gram_tiles(lhs, rhs, first, width, put):
    def body(i, _):
        left = lhs[:, pl.ds(pl.multiple_of(i * 256, 256), 256)]
        right = rhs[:, first : first + width]
        tile = lax.dot_general(left, right, (((0,), (0,)), ((), ())), preferred_element_type=F32)
        put(i, tile)
        return _

    lax.fori_loop(0, 4, body, 0)


def kernel(
    half_ints, out_ref, raw, x_ref, mate_x, got, mate_got, left, left_4,
    da, db, dc0, e, q0, q1, q2, q3, q4, v2, u2, w2,
    da_r, db_r, dc0_r, e_r, q0_r, q1_r, q2_r, q3_r, q4_r, v2_r, u2_r, w2_r,
    e_own, e_near, e_sum, fc, fc_r, gc, gc_r, h4, h4_r,
    tile_y, tile_y_r, tile, mix, mix_b, mix_r, summed, pieces, diag, diag_sum, diag_y, diag_z, diag_x,
    da_s, da_t, db_s, db_t, dc0_s, dc0_t, e_s, e_t,
    q0_s, q0_t, q1_s, q1_t, q2_s, q2_t, q3_s, q3_t, q4_s, q4_t, v2_s, v2_t, u2_s, u2_t, w2_s, w2_t,
    raw_t, x_s, x_t, mate_s, mate_t, near_s, near_t, ty_s, ty_t, mix_s, mix_t, piece_s, piece_t, piece0_s, piece0_t,
    dgy_s, dgy_t, dgz_s, dgz_t, fc_s, fc_t, h4_s, h4_t,
):
    raw_copies = [pltpu.make_async_copy(half_ints.at[p], raw.at[p], raw_t.at[p]) for p in range(3)]
    for copy in raw_copies:
        copy.start()
    a = lax.axis_index("aux")
    r = lax.axis_index("rows")
    z, y, l = a // 8, (a // 2) % 4, a % 2
    h, c = r // 2, r % 2
    x = 2 * h + l

    def dev(x_, y_, z_, c_):
        return (z_ * 8 + y_ * 2 + x_ % 2, 2 * (x_ // 2) + c_)

    def on_x(step):
        return dev(lax.rem(x + step, 4), y, z, c)

    def on_y(step):
        return dev(x, lax.rem(y + step, NY), z, c)

    def on_z(step):
        return dev(x, y, lax.rem(z + step, NZ), c)

    mate = dev(x, y, z, 1 - c)

    barrier = pltpu.get_barrier_semaphore()
    partners = [mate, on_x(1), on_x(3), on_y(1), on_y(3), on_z(1), on_z(7)]
    for partner in partners:
        pl.semaphore_signal(barrier, inc=1, device_id=partner, device_id_type=MESH)
    whole = OCC // 16 * 16
    for p in range(3):
        raw_copies[p].wait()

        def body(t, _, p=p):
            rows = pl.multiple_of(t * 16, 16)
            x_ref[pl.ds(p * 512 + rows, 16), :] = raw[p, pl.ds(rows, 16), :]
            return _

        lax.fori_loop(0, whole // 16, body, 0)
        tail = jnp.zeros((512 - OCC, W), BF)
        x_ref[p * 512 + whole : p * 512 + 512, :] = jnp.concatenate([raw[p, whole:OCC, :], tail], axis=0)
    pl.semaphore_wait(barrier, len(partners))

    def remote(src, dst, send, recv, device):
        return pltpu.make_async_remote_copy(
            src_ref=src, dst_ref=dst, send_sem=send, recv_sem=recv, device_id=device, device_id_type=MESH
        )

    def columns_of(h_, k):
        block = h_ * lax.rem(z + ORDER[k], NZ) + (1 - h_) * k
        return pl.ds(pl.multiple_of(block * 128, 128), 128)

    def x_copy(k, n, step):
        target_h = lax.rem(x + step, 4) // 2
        rows = pl.ds(pl.multiple_of(target_h * KH, KH), KH)
        columns = columns_of(h, k)
        return remote(x_ref.at[rows, columns], got.at[h, :, columns], x_s.at[n, k], x_t.at[h, k], on_x(step))

    arrived = set()

    def x_wait(slot, *ks):
        for k in ks:
            if (slot, k) in arrived:
                continue
            arrived.add((slot, k))
            columns = columns_of(slot, k)
            remote(x_ref.at[pl.ds(0, KH), columns], got.at[slot, :, columns], x_s.at[0, k], x_t.at[slot, k], mate).wait_recv()

    x_copies = [x_copy(k, n, step) for k in range(NZ) for n, step in enumerate((1, 3))]
    for copy in x_copies:
        copy.start()
    mate_copy = remote(x_ref, mate_x, mate_s.at[5], mate_t.at[5], mate)
    mate_copy.start()

    def z_ring(*refs):
        return Ring(NZ, z, lambda p: dev(x, y, p, c), *refs)

    def y_ring(*refs):
        return Ring(NY, y, lambda p: dev(x, p, z, c), *refs)

    ring_a = y_ring(da, da_r, da_s, da_t)
    ring_b = y_ring(db, db_r, db_s, db_t)
    rings_c = [
        z_ring(dc0, dc0_r, dc0_s, dc0_t),
    ]
    ring_e = z_ring(e, e_r, e_s, e_t)
    rings = [
        z_ring(q0, q0_r, q0_s, q0_t),
        z_ring(q1, q1_r, q1_s, q1_t),
        z_ring(q2, q2_r, q2_s, q2_t),
        z_ring(q3, q3_r, q3_s, q3_t),
    ]
    ring_4 = y_ring(q4, q4_r, q4_s, q4_t)
    rings_early = [y_ring(v2, v2_r, v2_s, v2_t), y_ring(u2, u2_r, u2_s, u2_t), y_ring(w2, w2_r, w2_s, w2_t)]

    def no_diagonal(i, first, tile_):
        ahead = lax.broadcasted_iota(jnp.int32, tile_.shape, 1) - lax.broadcasted_iota(jnp.int32, tile_.shape, 0)
        on_diagonal = ahead == i * 256 - first
        diag[:, first : first + tile_.shape[1]] += jnp.sum(jnp.where(on_diagonal, tile_, 0.0), axis=0, keepdims=True)
        return jnp.where(on_diagonal, 0.0, tile_)

    def put_y(ref, columns, i, tile_):
        tile_ = tile_.astype(BF)
        for k in range(2):
            zi = 2 * i + k
            for yi in range(4):
                rows = tile_[k * 128 + yi * 32 : k * 128 + yi * 32 + 32]
                ref[yi, zi // 4, zi % 4, :, columns] = rows

    def put_a(i, tile_):
        put_y(da, slice(0, CA), i, no_diagonal(i, CZ, tile_))

    def put_c(n):
        def put(i, tile_):
            tile_ = no_diagonal(i, n * CW, tile_).astype(BF)
            for k in range(2):
                for yi in range(4):
                    rings_c[n].buf[2 * i + k, yi // 2, yi % 2] = tile_[k * 128 + yi * 32 : k * 128 + yi * 32 + 32]

        return put

    def put_ea(n, side, total):
        e_own[side, n, 0, :, 0:CA] = total.astype(BF)

    def put_eb(n, side, total):
        e_own[side, n, 0, :, CA:EH] = total[:, 0 : EH - CA].astype(BF)
        e_own[side, n, 1] = total[:, EH - CA : W].astype(BF)

    def put_fc(k):
        def put(n, side, total):
            fc[n, :, k * CW : k * CW + CW] = total.astype(BF)

        return put

    def put_e(half, part, total):
        e_sum[half] = total

    def mate_part(p):
        columns = pl.ds(FROM[p], FROM[p + 1] - FROM[p])
        return remote(got.at[0, :, columns], mate_got.at[:, columns], mate_s.at[p], mate_t.at[p], mate)

    def turn(p, which):
        size = FROM[p + 1] - FROM[p]
        ref = left.at[p] if p < 3 else left_4.at[p - 3]
        columns = slice(FROM[p], FROM[p + 1])
        rows = (mate_got[:, columns] if which else got[0, :, columns]).T
        for yi in range(4):
            for k in range(size // 128):
                at = which * size + yi * (size // 4) + k * 32
                ref[at : at + 32, :] = rows[k * 128 + yi * 32 : k * 128 + yi * 32 + 32]

    def cross(p, *ks):
        size = FROM[p + 1] - FROM[p]
        for k in ks:
            block = lax.rem(z + ORDER[k], NZ)
            right = got[1, :, pl.ds(pl.multiple_of(block * 128, 128), 128)]
            rows = left[p] if p < 3 else left_4[p - 3]
            product = lax.dot_general(rows, right, (((1,), (0,)), ((), ())), preferred_element_type=F32).astype(BF)
            for which in range(2):
                if p != EARLY:
                    rings[p].buf[block, which, 0] = product[which * size : which * size + size]
                    continue
                i = max(i for i in range(3) if SPLITS[i] <= k)
                for yi in range(4):
                    at = which * size + yi * 64
                    rings_early[i].buf[yi, which, k - SPLITS[i]] = product[at : at + 64]

    def cross_4(which):
        rows = left_4[1, which * 128 : which * 128 + 128]
        for j in range(4):
            right = got[1, :, j * 256 : j * 256 + 256]
            product = lax.dot_general(rows, right, (((1,), (0,)), ((), ())), preferred_element_type=F32).astype(BF)
            for yi in range(4):
                for n in range(2):
                    q4[yi, which, 2 * j + n] = product[yi * 32 : yi * 32 + 32, n * 128 : n * 128 + 128]

    def put_early(first, count):
        def put(n, side, total):
            k = first + n % count
            ahead = 0
            for i, step in enumerate(ORDER):
                ahead = ahead + step * jnp.where(k == i, 1, 0)
            rings[EARLY].buf[lax.rem(z + ahead, NZ), n // count, 0] = total.astype(BF)

        return put

    def put_tile_early(which, side, total):
        tile[EARLY, c * (1 - which) + (1 - c) * which] = total

    def put_h4(n, side, total):
        h4[n % 8, n // 8] = total.astype(BF)

    def direct(src, dst, send, recv, size, pos, step_to):
        copies = []
        for d in range(1, size):
            copies.append(
                remote(src.at[lax.rem(pos + d, size)], dst.at[d - 1], send.at[d - 1], recv.at[d - 1], step_to(d))
            )
            copies[-1].start()
        return copies

    def over_y(p):
        def put(which, yi, total):
            if p < 3:
                tile_y[p, yi, which] = total.astype(BF)
            else:
                tile_y[p, yi, which, 0:32] = total.astype(BF)

        rings[p].finish(put, 4)
        rows = slice(0, 64 if p < 3 else 32)
        return direct(tile_y.at[p, :, :, rows], tile_y_r.at[p, :, :, rows], ty_s.at[p], ty_t.at[p], NY, y, on_y)

    def over_x(p, copies):
        for copy in copies:
            copy.wait_recv()
        rows = slice(0, 64 if p < 3 else 32)
        for which in range(2 if p != EARLY else 0):
            total = tile_y[p, y, which, rows].astype(F32)
            for d in range(NY - 1):
                total = total + tile_y_r[p, d, which, rows].astype(F32)
            tile[p, c if which == 0 else 1 - c, rows] = total
        if p == 3:
            received("h4")
            for which in range(2):
                total = h4[z, which].astype(F32)
                for d in range(NZ - 1):
                    total = total + h4_r[d, which].astype(F32)
                tile[p, c if which == 0 else 1 - c, 32:64] = total
        flipped = jnp.concatenate([tile[p, 0], tile[p, 1]], axis=0).T
        for side in range(2):
            for n in range(4):
                at = (n % 2) * 32 + side * 16
                mix[p, 2 + side, n] = tile[p, n // 2, at : at + 16, :]
                at = n * 32 + side * 16
                mix[p, side, n] = flipped[at : at + 16]
        mix_b[p] = mix[p].astype(BF)
        out = []
        for d in (1, 2, 3):
            sems = mix_s.at[p, d - 1], mix_t.at[p, d - 1]
            out.append(remote(mix_b.at[p, lax.rem(x + d, 4)], mix_r.at[p, d - 1], *sems, on_x(d)))
            out[-1].start()
        return out

    def collect(p, copies):
        for copy in copies:
            copy.wait_recv()
        for n in range(4):
            total = mix[p, x, n] + mix_r[p, 0, n].astype(F32)
            total = -0.5 * (total + (mix_r[p, 1, n].astype(F32) + mix_r[p, 2, n].astype(F32)))

            @pl.when(h == 1)
            def _(total=total, n=n):
                summed[p // 2, 4 * (p % 2) + n % 2 * 2 + n // 2] = total.astype(BF)

            @pl.when(h == 0)
            def _(total=total, n=n):
                at = (p % 2) * 64
                for b in range(2):
                    summed[p // 2, n * 2 + b, :, at : at + 64] = total[:, b * 64 : b * 64 + 64].astype(BF)

    ring_of = {"A": ring_a, "B": ring_b, "E": ring_e, "Q": ring_4}
    ring_of.update({f"C{i}": ring for i, ring in enumerate(rings_c)})
    ring_of.update({f"R{i}": ring for i, ring in enumerate(rings)})
    ring_of.update({f"{i}{EARLY}": ring for i, ring in zip("VUW", rings_early)})
    sent = {}
    task = {}
    near = dev(2 * h + (1 - l), y, z, c)
    mine = y * 2 + c

    def do(f):
        task[f.__name__.rstrip("_")] = f
        return f

    def received(name):
        for copy in sent[name]:
            copy.wait_recv()

    def start(name, *copies):
        sent[name] = copies
        for copy in copies:
            copy.start()

    def gC(n):
        if n == 0:
            diag[...] = jnp.zeros_like(diag)
        gram_tiles(x_ref, x_ref, n * CW, CW, put_c(n))

    for n in range(CZ // CW):
        task[f"gC{n}"] = functools.partial(gC, n)

    @do
    def gA():
        gram_tiles(x_ref, x_ref, CZ, CA, put_a)

    @do
    def gB0():
        mate_copy.wait_recv()
        gram_tiles(mate_x, x_ref, 0, 512, lambda i, tile_: put_y(db, slice(0, 512), i, tile_))

    @do
    def gB1():
        gram_tiles(mate_x, x_ref, 512, 512, lambda i, tile_: put_y(db, slice(512, 1024), i, tile_))

    @do
    def dgy():
        start("dgy", *[remote(diag, diag_y.at[d - 1], dgy_s.at[d - 1], dgy_t.at[d - 1], on_y(d)) for d in range(1, NY)])

    @do
    def dgz():
        received("dgy")
        diag_sum[...] = (diag[...] + diag_y[0]) + (diag_y[1] + diag_y[2])
        start(
            "dgz",
            *[remote(diag_sum, diag_z.at[d - 1], dgz_s.at[d - 1], dgz_t.at[d - 1], on_z(d)) for d in range(1, NZ)],
        )

    @do
    def fcs():
        sent["fc"] = direct(fc, fc_r, fc_s, fc_t, NY, y, on_y)

    @do
    def Ex():
        start("Ex", remote(e_own.at[1 - l], e_near, near_s.at[0], near_t.at[0], near))

    @do
    def Ea():
        received("Ex")

        def add_near(t, _):
            n, half = t // 2, t % 2
            total = e_own[l, n, half].astype(F32) + e_near[n, half].astype(F32)
            e[n, half, 0] = total.astype(BF)
            return _

        lax.fori_loop(0, 16, add_near, 0)

    @do
    def G():
        received("fc")
        total = fc[y].astype(F32)
        for d in range(NY - 1):
            total = total + fc_r[d].astype(F32)
        gc[0] = total[0:16]
        gc[1] = total[16:32]
        received("dgz")
        total = diag_sum[...]
        for d in range(NZ - 1):
            total = total + diag_z[d]
        diag_x[0] = total
        start(
            "G",
            remote(gc.at[1 - l], gc_r, near_s.at[1], near_t.at[1], near),
            remote(diag_x.at[0], diag_x.at[1], near_s.at[2], near_t.at[2], near),
        )

    @do
    def Ef():
        received("G")
        ring_e.finish(put_e)
        row = lax.broadcasted_iota(jnp.int32, (16, W), 0) + (z * 128 + y * 32 + l * 16)
        on_diagonal = lax.broadcasted_iota(jnp.int32, (16, W), 1) == row
        total = jnp.concatenate([gc[l] + gc_r[...], e_sum[0, :, 0:CA]], axis=1)
        out_ref[2 * h + c] = -0.5 * (total + jnp.where(on_diagonal, diag_x[0] + diag_x[1], 0.0))
        out_ref[2 * h + 1 - c] = -0.5 * jnp.concatenate([e_sum[0, :, CA:EH], e_sum[1]], axis=1)

    def row_piece(n):
        src = summed.at[n // 4, n % 4 * 2 : n % 4 * 2 + 2]
        return remote(src, pieces.at[z], piece_s.at[n], piece_t.at[z], dev(x, y, n, c))

    def row_wait(n):
        src = summed.at[n // 4, n % 4 * 2 : n % 4 * 2 + 2]
        return remote(src, pieces.at[n], piece_s.at[n], piece_t.at[n], dev(x, y, n, c))

    def column_piece(q, d):
        n = lax.rem(mine + d, 8)
        sems = piece0_s.at[q, d - 1], piece0_t.at[q, d - 1]
        return remote(summed.at[q, n], pieces.at[mine, q], *sems, dev(x, n // 2, z, n % 2))

    def send_pieces(q):
        @pl.when(h == 1)
        def _():
            for n in range(4 * q, 4 * q + 4):

                @pl.when(n != z)
                def _(n=n):
                    row_piece(n).start()

                @pl.when(n == z)
                def _(n=n):
                    pieces[n] = summed[q, n % 4 * 2 : n % 4 * 2 + 2]

        @pl.when(h == 0)
        def _():
            for d in range(1, 8):
                column_piece(q, d).start()
            pieces[mine, q] = summed[q, mine]

    task["pieces0"] = lambda: send_pieces(0)
    task["pieces1"] = lambda: send_pieces(1)

    @do
    def out():
        @pl.when(h == 1)
        def _():
            for n in range(8):

                @pl.when(n != z)
                def _(n=n):
                    row_wait(n).wait()

            for s in range(2):
                for n in range(8):
                    out_ref[s, :, n * 128 : n * 128 + 128] = pieces[n, s].astype(F32)

        @pl.when(h == 0)
        def _():
            for q in range(2):
                for d in range(1, 8):
                    column_piece(q, d).wait()
                for s in range(2):
                    for n in range(4):
                        parts = [pieces[v * 2 + s, q].astype(F32)[:, n * 32 : n * 32 + 32] for v in range(4)]
                        at = q * 512 + n * 128
                        out_ref[2 + s, :, at : at + 128] = jnp.concatenate(parts, axis=1)

    task["Af"] = lambda: ring_a.finish(put_ea, 2)
    task["Bf"] = lambda: ring_b.finish(put_eb, 2)
    for n, letter in enumerate("VUW"):
        count = SPLITS[n + 1] - SPLITS[n]
        task[f"{letter}{EARLY}f"] = functools.partial(rings_early[n].finish, put_early(SPLITS[n], count))
    task[f"Y{EARLY}"] = lambda: rings[EARLY].finish(put_tile_early)

    @do
    def Cf():
        for n, ring in enumerate(rings_c):
            ring.finish(put_fc(n))


    for name, ring in ring_of.items():
        for i in range(ring.size - 1):
            task[f"{name}.{i}"] = functools.partial(ring.step, i)

    def part_tasks(p):
        def send():
            x_wait(0, *range(FROM[p] // 128, FROM[p + 1] // 128))
            start(f"mp{p}", mate_part(p))

        def turn_mate():
            received(f"mp{p}")
            turn(p, 1)

        def cross_group(ks):
            x_wait(1, *ks)
            cross(p, *ks)

        def sum_y():
            sent[f"Y{p}"] = over_y(p)

        def sum_x():
            sent[f"X{p}"] = over_x(p, sent[f"Y{p}"] if p != EARLY else ())

        task[f"sp{p}"] = send
        task[f"tu{p}.0"] = lambda: turn(p, 0)
        task[f"tu{p}.1"] = turn_mate
        if p == 4:
            return
        for d, ks in enumerate(GROUPS):
            task[f"cr{p}.{d}"] = functools.partial(cross_group, ks)
        if p != EARLY:
            task[f"Y{p}"] = sum_y
        task[f"X{p}"] = sum_x
        task[f"K{p}"] = lambda: collect(p, sent[f"X{p}"])
        if p == EARLY:
            for n, letter in enumerate("VUW"):
                task[f"c{letter}{EARLY}"] = functools.partial(cross_group, tuple(range(SPLITS[n], SPLITS[n + 1])))

    for p in range(5):
        part_tasks(p)

    def last_part(which):
        x_wait(1, *range(NZ))
        cross_4(which)

    task["c4.0"] = lambda: last_part(0)
    task["c4.1"] = lambda: last_part(1)

    @do
    def Qf():
        ring_4.finish(put_h4)
        sent["h4"] = direct(h4, h4_r, h4_s, h4_t, NZ, z, on_z)

    for name in SCHEDULE:
        task[name]()
    for ring in ring_of.values():
        ring.drain()
    for copy in x_copies + [mate_copy]:
        copy.wait_send()
    for copies in sent.values():
        for copy in copies:
            copy.wait_send()
    out()


def shards(half_ints):
    dma = pltpu.SemaphoreType.DMA
    vmem = pltpu.VMEM
    bufs = [(NY, 2, 4, 32, CA), (NY, 2, 4, 32, W)] + [(NZ, 2, 2, 32, CW)] * (CZ // CW) + [(NZ, 2, 1, 16, EH)]
    bufs += [(NZ, 2, 1, 64 if p == EARLY else 256, 128) for p in range(3)]
    bufs += [(NZ, 2, 1, 128, 128), (NY, 2, 8, 32, 128)]
    bufs += [(NY, 2, SPLITS[i + 1] - SPLITS[i], 64, 128) for i in range(3)]
    scratch = [vmem((3, OCC, W), BF), vmem((K, W), BF), vmem((K, W), BF)]
    scratch += [vmem((2, KH, W), BF), vmem((KH, W), BF), vmem((3, 512, KH), BF), vmem((2, 256, KH), BF)]
    scratch += [vmem(shape, BF) for shape in bufs]
    scratch += [vmem((2, shape[0] - 1) + shape[2:], BF) for shape in bufs]
    scratch += [
        vmem((2, NZ, 2, 16, EH), BF),
        vmem((NZ, 2, 16, EH), BF),
        vmem((2, 16, EH), F32),
        vmem((NY, 32, CZ), BF),
        vmem((NY - 1, 32, CZ), BF),
        vmem((2, 16, CZ), F32),
        vmem((16, CZ), F32),
        vmem((NZ, 2, 32, 128), BF),
        vmem((NZ - 1, 2, 32, 128), BF),
        vmem((PARTS, NY, 2, 64, 128), BF),
        vmem((PARTS, NY - 1, 2, 64, 128), BF),
        vmem((PARTS, 2, 64, 128), F32),
        vmem((PARTS, 4, 4, 16, 128), F32),
        vmem((PARTS, 4, 4, 16, 128), BF),
        vmem((PARTS, 3, 4, 16, 128), BF),
        vmem((2, 8, 16, 128), BF),
        vmem((8, 2, 16, 128), BF),
        vmem((1, W), F32),
        vmem((1, W), F32),
        vmem((NY - 1, 1, W), F32),
        vmem((NZ - 1, 1, W), F32),
        vmem((2, 1, W), F32),
    ]
    for shape in bufs:
        scratch += [dma((2, shape[0] - 1))] * 2
    scratch += [dma((3,))] + [dma((2, NZ))] * 2 + [dma((6,))] * 2 + [dma((3,))] * 2
    scratch += [dma((PARTS, NY - 1))] * 2 + [dma((PARTS, 3))] * 2 + [dma((NZ,))] * 2 + [dma((2, 7))] * 2
    scratch += [dma((NY - 1,))] * 2 + [dma((NZ - 1,))] * 2 + [dma((NY - 1,))] * 2 + [dma((NZ - 1,))] * 2
    out = pl.pallas_call(
        kernel,
        out_shape=jax.ShapeDtypeStruct((4, 16, W), F32),
        in_specs=[pl.BlockSpec(memory_space=pl.ANY)],
        out_specs=pl.BlockSpec(memory_space=pltpu.VMEM),
        scratch_shapes=scratch,
        compiler_params=pltpu.CompilerParams(
            collective_id=0, has_side_effects=True, vmem_limit_bytes=56 * 1024 * 1024
        ),
        cost_estimate=pl.CostEstimate(flops=2 * 1024 * 1024 * K * 3, bytes_accessed=4 << 20, transcendentals=0),
    )(half_ints)
    return out.transpose(1, 0, 2)


def solution(mesh):
    placed = (P("aux", None, "rows"),)
    return jax.shard_map(
        shards, mesh=mesh, in_specs=placed, out_specs=P("aux", None, "rows"), check_vma=False
    )
```
